128 devices in a mesh: row: 8 (over y, core), col: 16 (over z, x).
Axes of the slice: x: 4, y: 4, z: 4, core: 2. Of those that a mesh axis runs over, the one named last changes fastest.
Arguments:
- precip: float32 [2048, 8192], P('row', 'col'), may hold values from 0.002 to 0.02
- head: float32 [2048, 8192], P('row', 'col'), may hold values from -4 to 4
- trans_coef: float32 [2048, 8192], P('row', 'col'), may hold values from 0.05 to 0.5
- land: int32 [2048, 8192], P('row', 'col'), may hold values 0 or 1
- dest: int32 [2048, 64], P('row', 'col'), may hold values from 0 to 131071, as said below
- moisture: float32 [131072, 16, 128], P(('row', 'col')), may hold values from 0.08 to 0.42
- ksat: float32 [131072, 128], P(('row', 'col')), may hold values from 0.002 to 0.01
Outputs:
- saturation: float32 [131072, 16, 128], P(('row', 'col'))
- head_new: float32 [2048, 8192], P('row', 'col')
The draws below stay inside these ranges and needn't reach their ends.
Inputs may be any that keep to these rules, and one draw needn't show every extreme that they name: dest is a permutation of 0 .. 131071; its value is an owner's index along row+col times 1024 plus a slot. At most 16 blocks of one device's tile go to one owner, and every device sends exactly 16 to some owner; every owner receives 1024 blocks.
All inputs are finite; a program needn't handle non-finite values. No bound on the sum of `land` on one device may be relied on, other than what follows from the above.
Results may differ from the reference program's by a relative error of at most 0.00002.
Values sent between devices are 32-bit elements; how exact they have to be, the bound alone decides.
No kernel may reach another device: no remote copies, remote signals or barrier semaphores. Data moves between devices by JAX's collectives and lax.ppermute only.
A program may use at most 192 MiB of HBM per device.

```python
import math
import jax
import jax.numpy as jnp

L = 16
TR = 256
TC = 512
SWEEPS = 4
SLOTS = 1024
CAP = 16
NR = 2048
NC = 8192
NBLK = 131072
N_ROW = 8
N_COL = 16


def permuted_slot_list(subkey):
    return jax.random.permutation(subkey, SLOTS)


def draw_dest(key, part):
    processor_units = N_ROW * N_COL
    tickets_total = processor_units * CAP
    key_shuffle, key_leading, key_local, slot_key_random = jax.random.split(key, 4)
    tickets = jnp.arange(tickets_total, dtype=jnp.int32) // CAP
    shuffled = jax.random.permutation(key_shuffle, tickets)
    leading = jax.random.randint(key_leading, (), 0, processor_units, dtype=jnp.int32)
    scores = (shuffled != leading).astype(jnp.int32) * tickets_total + jnp.arange(tickets_total, dtype=jnp.int32)
    ranking = jnp.argsort(scores)
    shifts = shuffled[ranking[:SLOTS]]
    worker_rank_here = jax.vmap(permuted_slot_list)(jax.random.split(key_local, processor_units))
    relabel_blocks = jax.vmap(permuted_slot_list)(jax.random.split(slot_key_random, processor_units))
    sources = jnp.arange(processor_units, dtype=jnp.int32)[:, None]
    block_owner_list = (sources + shifts[worker_rank_here]) % processor_units
    slot_number = relabel_blocks[block_owner_list, worker_rank_here]
    target = block_owner_list * SLOTS + slot_number
    layout = target.reshape(N_ROW, N_COL, TR, TC // 128).transpose(0, 2, 1, 3)
    return layout.reshape(NR, NC // 128).astype(jnp.int32)


def place_ends(result, own_key, least, largest):
    shape = result.shape
    spot = [jax.random.randint(jax.random.fold_in(own_key, axis), (), 0, shape[axis]) for axis in range(len(shape))]
    result = result.at[tuple(spot)].set(least)
    longest = shape.index(max(shape))
    spot[longest] = (spot[longest] + 1) % shape[longest]
    return result.at[tuple(spot)].set(largest)


def block_scale(key, extent, shards, least, high):
    gain, own = 1.0, jax.random.fold_in(key, 6)
    for position, parts in shards:
        heights = jnp.exp(jax.random.uniform(jax.random.fold_in(own, position), (parts,), jnp.float32, least / len(shards), high / len(shards)))
        gain = gain * jnp.repeat(heights, extent[position] // parts).reshape([-1 if axis == position else 1 for axis in range(len(extent))])
    return gain


def gaussian(key, dims, deviation, most, cuts=(), kind=jnp.bfloat16):
    gain = block_scale(key, dims, cuts, -0.22, 0.18) if cuts else 1.0
    entries = jax.random.normal(key, dims, jnp.float32) * deviation * gain
    return jnp.minimum(jnp.maximum(entries, -most), most).astype(kind)


def setup_inputs(seed: int = 0) -> dict:
    key_of = jax.random.split(jax.random.key(seed), 8)
    precip = jnp.clip(jnp.exp(math.log(0.02) - 2.30258502 * jax.random.uniform(key_of[0], (NR, NC), jnp.float32) ** block_scale(key_of[0], (NR, NC), ((0, 8), (1, 16)), -0.2, 0.2)), 0.002, 0.02)
    head = gaussian(key_of[1], (NR, NC), 1.0, 4.0, ((0, 8), (1, 16)), jnp.float32)
    trans_coef = jnp.clip(jnp.exp(math.log(0.5) - 2.3025851 * jax.random.uniform(key_of[2], (NR, NC), jnp.float32) ** block_scale(key_of[2], (NR, NC), ((0, 8), (1, 16)), -0.2, 0.2)), 0.05, 0.5)
    land = place_ends((jax.random.randint(key_of[3], (NR, NC), 0, 4) < 3).astype(jnp.int32), jax.random.fold_in(key_of[3], 1), 0, 1)
    dest = draw_dest(jax.random.fold_in(key_of[7], 71), 0)
    moisture = jnp.clip(0.08 + 0.3399999886751175 * jax.random.uniform(key_of[5], (NBLK, L, 128), jnp.float32) ** block_scale(key_of[5], (NBLK, L, 128), ((0, 128),), -0.2, 0.2), 0.08, 0.42)
    ksat = jnp.clip(jnp.exp(math.log(0.01) - 1.6094378 * jax.random.uniform(key_of[6], (NBLK, 128), jnp.float32) ** block_scale(key_of[6], (NBLK, 128), ((0, 128),), -0.2, 0.2)), 0.002, 0.01)
    return {"precip": precip, "head": head, "trans_coef": trans_coef, "land": land, "dest": dest, "moisture": moisture, "ksat": ksat}


layer_depth = 0.1
step_ratio = 0.1
residual_water = 0.05
pore_range = 0.4
diff_length = 0.5
couple_rate = 0.05
recharge_gain = 20.0
store_rate = 0.2


def factor(moisture, ksat):
    layers = moisture.shape[1]
    depths = (jnp.arange(layers, dtype=jnp.float32) + 0.5) * layer_depth
    scaled_k = ksat[:, None, :] * jnp.exp(-depths)[None, :, None]
    wetness = (moisture - residual_water) / pore_range
    conduct = scaled_k * wetness * wetness * wetness
    slopes = 3.0 * scaled_k * wetness * wetness / pore_range
    diffusion = scaled_k * diff_length * (0.2 + wetness * wetness)
    coupling = (diffusion[:, :-1] + diffusion[:, 1:]) / (2.0 * layer_depth)
    subs, pivots, ratios = [], [], []
    for k in range(layers):
        diagonal = step_ratio + jnp.zeros_like(moisture[:, k])
        if k > 0:
            diagonal = diagonal + coupling[:, k - 1]
        if k < layers - 1:
            diagonal = diagonal + coupling[:, k]
        if k == 0:
            diagonal = diagonal + 0.5 * slopes[:, 0]
        if k == layers - 1:
            diagonal = diagonal + 0.5 * slopes[:, k] + couple_rate
        if k > 0:
            sub_term = -(0.5 * slopes[:, k - 1] + coupling[:, k - 1])
            pivot_k = diagonal - sub_term * ratios[k - 1]
        else:
            sub_term = jnp.zeros_like(diagonal)
            pivot_k = diagonal
        if k < layers - 1:
            ratio_k = (0.5 * slopes[:, k + 1] - coupling[:, k]) / pivot_k
        else:
            ratio_k = jnp.zeros_like(diagonal)
        subs.append(sub_term)
        pivots.append(pivot_k)
        ratios.append(ratio_k)
    return conduct, slopes, coupling, subs, pivots, ratios


def solve(moisture, factors, infiltration, owned_head):
    conduct, slopes, coupling, subs, pivots, ratios = factors
    layers = moisture.shape[1]
    face_flux = 0.5 * (conduct[:, :-1] + conduct[:, 1:]) - coupling * (moisture[:, 1:] - moisture[:, :-1])
    table = residual_water + pore_range * jax.nn.sigmoid(owned_head)
    bottom = conduct[:, -1] + couple_rate * (moisture[:, -1] - table)
    reduced = []
    for k in range(layers):
        above = infiltration if k == 0 else face_flux[:, k - 1]
        below = bottom if k == layers - 1 else face_flux[:, k]
        right_side = above - below
        if k > 0:
            right_side = right_side - subs[k] * reduced[k - 1]
        reduced.append(right_side / pivots[k])
    change = [None] * layers
    change[layers - 1] = reduced[layers - 1]
    for k in range(layers - 2, -1, -1):
        change[k] = reduced[k] - ratios[k] * change[k + 1]
    updated = moisture + jnp.stack(change, axis=1)
    saturation = (updated - residual_water) / pore_range
    recharge = bottom + (slopes[:, -1] + couple_rate) * change[layers - 1]
    return saturation, recharge


def relax(source_term, trans_pad, head_pad, land_share):
    center_t = trans_pad[1:-1, 1:-1]
    face_up = 0.5 * (center_t + trans_pad[:-2, 1:-1])
    face_down = 0.5 * (center_t + trans_pad[2:, 1:-1])
    face_left = 0.5 * (center_t + trans_pad[1:-1, :-2])
    face_right = 0.5 * (center_t + trans_pad[1:-1, 2:])
    total_t = face_up + face_down + face_left + face_right
    inflow = face_up * head_pad[:-2, 1:-1] + face_down * head_pad[2:, 1:-1]
    inflow = inflow + face_left * head_pad[1:-1, :-2] + face_right * head_pad[1:-1, 2:]
    return (source_term + inflow) / (store_rate + total_t) * land_share


def reference(precip, head, trans_coef, land, dest, moisture, ksat):
    grid_rows, grid_cols = precip.shape
    count = grid_rows * grid_cols // 128
    land_share = land.astype(jnp.float32)
    infiltration = (precip * land_share).reshape(count, 128)
    head_blocks = head.reshape(count, 128)
    target = dest.reshape(count)
    owned_infil = jnp.zeros_like(infiltration).at[target].set(infiltration)
    owned_head = jnp.zeros_like(head_blocks).at[target].set(head_blocks)
    factors = factor(moisture, ksat)
    saturation, recharge = solve(moisture, factors, owned_infil, owned_head)
    tile_recharge = recharge[target].reshape(grid_rows, grid_cols)
    initial = head * land_share
    transmit = trans_coef * (1.0 + 0.5 * jnp.tanh(head))
    source_term = store_rate * initial + recharge_gain * tile_recharge
    trans_pad = jnp.pad(transmit, 1)
    surface = initial
    for sweep_k in range(SWEEPS):
        surface = relax(source_term, trans_pad, jnp.pad(surface, 1), land_share)
    return saturation, surface
```

```python
import math

import jax
import jax.numpy as jnp
from jax import lax
from jax.experimental import pallas as pl
from jax.experimental.pallas import tpu as pltpu
from jax.sharding import PartitionSpec as P

SWEEPS = 4
LANES = 128
EDGE = 8

layer_depth = 0.1
step_ratio = 0.1
residual_water = 0.05
pore_range = 0.4
couple_rate = 0.05
recharge_gain = 20.0
store_rate = 0.2

F32 = jnp.float32
BF16 = jnp.bfloat16
MIB = 1 << 20


def iota(shape, dim):
    return lax.broadcasted_iota(jnp.int32, shape, dim)


def params(mib):
    return pltpu.CompilerParams(vmem_limit_bytes=mib * MIB)


def cost(us):
    return pl.CostEstimate(flops=0, bytes_accessed=int(us * 3.0e6), transcendentals=0)


def halves(x):
    high = x.astype(BF16)
    low = (x - high.astype(F32)).astype(BF16)
    return high, low


def whole(count):
    return [pl.BlockSpec(memory_space=pltpu.VMEM)] * count


def pack_kernel(peers, cap, owned, dest_ref, precip_ref, head_ref, land_ref, out_ref, place_ref, hot_ref, data_ref):
    rows, cols = precip_ref.shape
    parts = cols // LANES
    blocks = rows * parts
    stride = 2 * cap + 1
    dest = dest_ref[...]
    shift = owned.bit_length() - 1
    owner = dest >> shift
    label = (dest & (owned - 1)) + 1
    owner_hot = owner == iota((peers, blocks), 0)
    before = (iota((LANES, LANES), 0) < iota((LANES, LANES), 1)).astype(F32).astype(BF16)
    carry = jnp.zeros((peers, 1), F32)
    ranks = []
    for chunk in range(blocks // LANES):
        hot = owner_hot[:, chunk * LANES : (chunk + 1) * LANES]
        hot_f = hot.astype(F32)
        count = jnp.dot(hot_f.astype(BF16), before, preferred_element_type=F32) + carry
        ranks.append(jnp.sum(count * hot_f, axis=0, keepdims=True))
        carry = carry + jnp.sum(hot_f, axis=1, keepdims=True)
    rank = jnp.concatenate(ranks, axis=1).astype(jnp.int32)
    place = owner + peers * rank
    place_f = place.astype(F32)
    eye = iota((LANES, LANES), 0) == iota((LANES, LANES), 1)
    for chunk in range(blocks // LANES):
        line = place_f[:, chunk * LANES : (chunk + 1) * LANES]
        place_ref[chunk * LANES : (chunk + 1) * LANES, :] = jnp.sum(
            jnp.where(eye, line, 0.0), axis=1, keepdims=True
        ).astype(jnp.int32)
    for part in range(parts):
        lane = slice(part * LANES, (part + 1) * LANES)
        line = slice(part * rows, (part + 1) * rows)
        infil = precip_ref[:, lane] * land_ref[:, lane].astype(F32)
        for at, piece in enumerate(halves(infil) + halves(head_ref[:, lane])):
            data_ref[line, at * LANES : (at + 1) * LANES] = piece
    for rank_k in range(cap):
        hot_ref[rank_k * peers : (rank_k + 1) * peers, :] = (
            (place == iota((peers, blocks), 0) + rank_k * peers).astype(F32).astype(BF16)
        )
    group = 8
    for first in range(0, cap, group):
        moved = jnp.dot(
            hot_ref[first * peers : (first + group) * peers, :], data_ref[...], preferred_element_type=F32
        )
        for k in range(group):
            part = moved[k * peers : (k + 1) * peers]
            out_ref[pl.ds(first + k, peers, stride=stride), :] = part[:, :LANES] + part[:, LANES : 2 * LANES]
            out_ref[pl.ds(cap + first + k, peers, stride=stride), :] = (
                part[:, 2 * LANES : 3 * LANES] + part[:, 3 * LANES :]
            )
    owner_f = owner_hot.astype(F32)
    rank_hot = (rank == iota((LANES, blocks), 0)).astype(F32).astype(BF16)
    contract = (((1,), (1,)), ((), ()))
    tops = (owner_f * (label >> 5).astype(F32)).astype(BF16)
    lows = (owner_f * (label & 31).astype(F32)).astype(BF16)
    labels = 32.0 * lax.dot_general(tops, rank_hot, contract, preferred_element_type=F32)
    labels = labels + lax.dot_general(lows, rank_hot, contract, preferred_element_type=F32)
    out_ref[pl.ds(2 * cap, peers, stride=stride), :] = labels


def pack(dest_row, precip, head, land, peers, cap, owned):
    blocks = dest_row.shape[1]

    def kernel(*refs):
        pack_kernel(peers, cap, owned, *refs)

    return pl.pallas_call(
        kernel,
        out_shape=(
            jax.ShapeDtypeStruct((peers * (2 * cap + 1), LANES), F32),
            jax.ShapeDtypeStruct((blocks, 1), jnp.int32),
        ),
        in_specs=whole(4),
        out_specs=tuple(whole(2)),
        scratch_shapes=[pltpu.VMEM((peers * cap, blocks), BF16), pltpu.VMEM((blocks, 4 * LANES), BF16)],
        compiler_params=params(40),
        cost_estimate=cost(5),
        name="pack_forcing",
    )(dest_row, precip, head, land)


def layer_terms(moist, half_k, depth_factor):
    wet = moist * (1.0 / pore_range) - residual_water / pore_range
    wet2 = wet * wet
    a = half_k * depth_factor
    t = a * wet2
    return wet, 7.5 * t, t * wet, a + 5.0 * t


def inverse(x):
    y = pl.reciprocal(x, approx=True)
    return y * (2.0 - x * y)


def eliminate(layers, load, ksat, infil, response, keep):
    half_k = 0.5 * ksat
    moist = load(0)
    wet, hs, hc, d5 = layer_terms(moist, half_k, math.exp(-0.5 * layer_depth))
    flux_above = infil
    ratio = reduced = resp = hs_prev = g_prev = None
    for k in range(layers):
        last = k == layers - 1
        if not last:
            moist_n = load(k + 1)
            wet_n, hs_n, hc_n, d5_n = layer_terms(
                moist_n, half_k, math.exp(-(k + 1.5) * layer_depth)
            )
            g = d5 + d5_n
            flux = (hc + hc_n) - g * (moist_n - moist)
        if k == 0:
            diagonal = (g + step_ratio) + hs
        elif last:
            diagonal = (g_prev + (step_ratio + couple_rate)) + hs
        else:
            diagonal = (g_prev + step_ratio) + g
        if last:
            bottom = 2.0 * hc + couple_rate * (moist - residual_water)
            right = flux_above - bottom
        else:
            right = (0.0 - flux) if flux_above is None else (flux_above - flux)
        if k == 0:
            inv = inverse(diagonal)
            reduced = right * inv
            resp = inv
        else:
            neg_sub = hs_prev + g_prev
            inv = inverse(diagonal + neg_sub * ratio)
            reduced = (right + neg_sub * reduced) * inv
            if response:
                resp = neg_sub * resp * inv
        if last:
            return bottom, 2.0 * hs + couple_rate, reduced, resp, inv, wet
        ratio = (hs_n - g) * inv
        if keep is not None:
            keep(k, wet, ratio, reduced)
        hs_prev, g_prev = hs, g
        flux_above = flux
        moist, wet, hs, hc, d5 = moist_n, wet_n, hs_n, hc_n, d5_n


def response_kernel(layers, chunk, moist_ref, ksat_ref, alpha_ref, beta_ref, gamma_ref):
    def step(j, carry):
        base = j * (chunk * layers)
        line = pl.ds(j * chunk, chunk)
        load = lambda k: moist_ref[pl.ds(base + k, chunk, stride=layers), :]
        bottom, gain, reduced, resp, inv, _ = eliminate(layers, load, ksat_ref[line, :], None, True, None)
        alpha_ref[line, :] = bottom + gain * reduced
        beta_ref[line, :] = gain * resp
        gamma_ref[line, :] = (couple_rate * pore_range) * (gain * inv - 1.0)
        return carry

    lax.fori_loop(0, ksat_ref.shape[0] // chunk, step, 0)


def response(moist2, ksat, layers):
    owned = ksat.shape[0]
    size = 128

    def kernel(*refs):
        response_kernel(layers, 32, *refs)

    small = pl.BlockSpec((size, LANES), lambda i: (i, 0))
    return pl.pallas_call(
        kernel,
        grid=(owned // size,),
        out_shape=(jax.ShapeDtypeStruct((owned, LANES), F32),) * 3,
        in_specs=[pl.BlockSpec((size * layers, LANES), lambda i: (i, 0)), small],
        out_specs=(small,) * 3,
        compiler_params=params(24),
        cost_estimate=cost(11),
        name="column_response",
    )(moist2, ksat)


def saturation_kernel(layers, chunk, moist_ref, ksat_ref, infil_ref, share_ref, out_ref, wet_s, ratio_s, reduced_s):
    def step(j, carry):
        base = j * (chunk * layers)
        line = pl.ds(j * chunk, chunk)
        load = lambda k: moist_ref[pl.ds(base + k, chunk, stride=layers), :]

        def keep(k, wet, ratio, reduced):
            wet_s[k] = wet
            ratio_s[k] = ratio
            reduced_s[k] = reduced

        _, _, reduced, _, inv, wet = eliminate(layers, load, ksat_ref[line, :], infil_ref[line, :], False, keep)
        change = reduced + (couple_rate * pore_range) * share_ref[line, :] * inv
        out_ref[pl.ds(base + layers - 1, chunk, stride=layers), :] = wet + (1.0 / pore_range) * change
        for k in range(layers - 2, -1, -1):
            change = reduced_s[k] - ratio_s[k] * change
            out_ref[pl.ds(base + k, chunk, stride=layers), :] = wet_s[k] + (1.0 / pore_range) * change
        return carry

    lax.fori_loop(0, ksat_ref.shape[0] // chunk, step, 0)


def saturate(moist2, ksat, infil, share, layers):
    owned = ksat.shape[0]
    size, chunk = 128, 32

    def kernel(*refs):
        saturation_kernel(layers, chunk, *refs)

    small = pl.BlockSpec((size, LANES), lambda i: (i, 0))
    large = pl.BlockSpec((size * layers, LANES), lambda i: (i, 0))
    return pl.pallas_call(
        kernel,
        grid=(owned // size,),
        out_shape=jax.ShapeDtypeStruct((owned * layers, LANES), F32),
        in_specs=[large, small, small, small],
        out_specs=large,
        scratch_shapes=[pltpu.VMEM((layers - 1, chunk, LANES), F32)] * 3,
        compiler_params=params(24),
        cost_estimate=cost(13),
        name="column_saturation",
    )(moist2, ksat, infil, share)


def owner_kernel(peers, cap, got_ref, alpha_ref, beta_ref, gamma_ref, infil_ref, share_ref, ans_ref, data_ref, hot_ref, back_ref, rech_ref):
    owned = alpha_ref.shape[0]
    stride = 2 * cap + 1
    labels = got_ref[pl.ds(2 * cap, peers, stride=stride), :]
    turned = jnp.transpose(labels).astype(jnp.int32) - 1
    labels = labels.astype(jnp.int32) - 1
    for k in range(cap):
        line = slice(k * peers, (k + 1) * peers)
        pieces = halves(got_ref[pl.ds(k, peers, stride=stride), :])
        pieces = pieces + halves(got_ref[pl.ds(cap + k, peers, stride=stride), :])
        for at, piece in enumerate(pieces):
            data_ref[line, at * LANES : (at + 1) * LANES] = piece
        hot_ref[:, line] = (turned[k : k + 1, :] == iota((owned, peers), 0)).astype(F32).astype(BF16)
        back_ref[line, :] = (labels[:, k : k + 1] == iota((peers, owned), 1)).astype(F32).astype(BF16)
    group = 512
    for first in range(0, owned, group):
        line = slice(first, first + group)
        moved = jnp.dot(hot_ref[line, :], data_ref[...], preferred_element_type=F32)
        infil = moved[:, :LANES] + moved[:, LANES : 2 * LANES]
        head = moved[:, 2 * LANES : 3 * LANES] + moved[:, 3 * LANES :]
        share = jax.nn.sigmoid(head)
        infil_ref[line, :] = infil
        share_ref[line, :] = share
        rech = alpha_ref[line, :] + beta_ref[line, :] * infil + gamma_ref[line, :] * share
        high, low = halves(rech)
        rech_ref[line, :LANES] = high
        rech_ref[line, LANES:] = low
    many = 8
    for first in range(0, cap, many):
        moved = jnp.dot(
            back_ref[first * peers : (first + many) * peers, :], rech_ref[...], preferred_element_type=F32
        )
        for k in range(many):
            part = moved[k * peers : (k + 1) * peers]
            ans_ref[pl.ds(first + k, peers, stride=cap), :] = part[:, :LANES] + part[:, LANES:]


def owner_side(got, alpha, beta, gamma, peers, cap):
    owned = alpha.shape[0]

    def kernel(*refs):
        owner_kernel(peers, cap, *refs)

    return pl.pallas_call(
        kernel,
        out_shape=(
            jax.ShapeDtypeStruct((owned, LANES), F32),
            jax.ShapeDtypeStruct((owned, LANES), F32),
            jax.ShapeDtypeStruct((peers * cap, LANES), F32),
        ),
        in_specs=whole(4),
        out_specs=tuple(whole(3)),
        scratch_shapes=[
            pltpu.VMEM((peers * cap, 4 * LANES), BF16),
            pltpu.VMEM((owned, peers * cap), BF16),
            pltpu.VMEM((peers * cap, owned), BF16),
            pltpu.VMEM((owned, 2 * LANES), BF16),
        ],
        compiler_params=params(48),
        cost_estimate=cost(8),
        name="owner_side",
    )(got, alpha, beta, gamma)


def put_sides(x, left_ref, right_ref, at):
    cols = x.shape[1]
    left_ref[at : at + EDGE, :] = jnp.transpose(x[:, :LANES])[:EDGE, :]
    right_ref[at : at + EDGE, :] = jnp.transpose(x[:, cols - LANES :])[LANES - EDGE :, :]


def source_kernel(peers, cap, back_ref, place_ref, initial_ref, source_ref, left_ref, right_ref, data_ref, hot_ref):
    rows, cols = initial_ref.shape
    blocks = place_ref.shape[0]
    place = place_ref[...]
    for k in range(cap):
        line = slice(k * peers, (k + 1) * peers)
        high, low = halves(back_ref[pl.ds(k, peers, stride=cap), :])
        data_ref[line, :LANES] = high
        data_ref[line, LANES:] = low
        hot_ref[:, line] = (place == iota((blocks, peers), 1) + k * peers).astype(F32).astype(BF16)
    for part in range(cols // LANES):
        lane = slice(part * LANES, (part + 1) * LANES)
        moved = jnp.dot(hot_ref[part * rows : (part + 1) * rows, :], data_ref[...], preferred_element_type=F32)
        source_ref[:, lane] = store_rate * initial_ref[:, lane] + recharge_gain * (
            moved[:, :LANES] + moved[:, LANES:]
        )
    put_sides(source_ref[...], left_ref, right_ref, 0)


def source_of(back, place, initial, peers, cap):
    rows, cols = initial.shape
    blocks = place.shape[0]

    def kernel(*refs):
        source_kernel(peers, cap, *refs)

    side = jax.ShapeDtypeStruct((EDGE, rows), F32)
    return pl.pallas_call(
        kernel,
        out_shape=(jax.ShapeDtypeStruct((rows, cols), F32), side, side),
        in_specs=whole(3),
        out_specs=tuple(whole(3)),
        scratch_shapes=[pltpu.VMEM((peers * cap, 2 * LANES), BF16), pltpu.VMEM((blocks, peers * cap), BF16)],
        compiler_params=params(32),
        cost_estimate=cost(4),
        name="tile_source",
    )(back, place, initial)


def derive_kernel(head_ref, trans_ref, land_ref, initial_ref, left_ref, right_ref, up_ref, down_ref, transmit_ref):
    rows = head_ref.shape[0]
    head = head_ref[...]
    share = land_ref[...].astype(F32)
    initial = head * share
    transmit = trans_ref[...] * (1.0 + 0.5 * jnp.tanh(head))
    initial_ref[...] = initial
    transmit_ref[...] = transmit
    for at, x in enumerate((initial, transmit, share)):
        put_sides(x, left_ref, right_ref, at * EDGE)
        up_ref[at * EDGE : (at + 1) * EDGE, :] = x[:EDGE, :]
        down_ref[at * EDGE : (at + 1) * EDGE, :] = x[rows - EDGE :, :]


def derive(head, trans_coef, land):
    rows, cols = head.shape
    tile = jax.ShapeDtypeStruct((rows, cols), F32)
    side = jax.ShapeDtypeStruct((3 * EDGE, rows), F32)
    line = jax.ShapeDtypeStruct((3 * EDGE, cols), F32)
    return pl.pallas_call(
        derive_kernel,
        out_shape=(tile, side, side, line, line, tile),
        in_specs=whole(3),
        out_specs=tuple(whole(6)),
        compiler_params=params(24),
        cost_estimate=cost(3),
        name="derive_tile",
    )(head, trans_coef, land)


def exchange(up_line, down_line, left_side, right_side):
    rows = left_side.shape[1]

    def ring(axis, by):
        count = lax.axis_size(axis)
        return [(i, (i + by) % count) for i in range(count)]

    from_left = lax.ppermute(right_side, "col", ring("col", 1))
    from_right = lax.ppermute(left_side, "col", ring("col", -1))
    down_send = jnp.concatenate([down_line, from_left[:, rows - LANES :], from_right[:, rows - LANES :]], axis=1)
    up_send = jnp.concatenate([up_line, from_left[:, :LANES], from_right[:, :LANES]], axis=1)
    from_above = lax.ppermute(down_send, "row", ring("row", 1))
    from_below = lax.ppermute(up_send, "row", ring("row", -1))
    return from_left, from_right, from_above, from_below


def left_block(side):
    return jnp.transpose(jnp.concatenate([jnp.zeros((LANES - EDGE, LANES), F32), side], axis=0))


def right_block(side):
    return jnp.transpose(jnp.concatenate([side, jnp.zeros((LANES - EDGE, LANES), F32)], axis=0))


def assemble(out_ref, tile, sides, at):
    from_left, from_right, from_above, from_below = sides
    rows, cols = tile.shape
    part = slice(at * EDGE, (at + 1) * EDGE)
    bottom = slice(EDGE + rows, 2 * EDGE + rows)
    right = slice(LANES + cols, 2 * LANES + cols)
    mid = slice(LANES, LANES + cols)
    out_ref[EDGE : EDGE + rows, mid] = tile
    out_ref[:EDGE, mid] = from_above[part, :cols]
    out_ref[bottom, mid] = from_below[part, :cols]
    for first in range(0, rows, LANES):
        line = slice(EDGE + first, EDGE + first + LANES)
        out_ref[line, :LANES] = left_block(from_left[part, first : first + LANES])
        out_ref[line, right] = right_block(from_right[part, first : first + LANES])
    out_ref[:EDGE, :LANES] = left_block(from_above[part, cols : cols + LANES])[LANES - EDGE :, :]
    out_ref[:EDGE, right] = right_block(from_above[part, cols + LANES :])[LANES - EDGE :, :]
    out_ref[bottom, :LANES] = left_block(from_below[part, cols : cols + LANES])[:EDGE, :]
    out_ref[bottom, right] = right_block(from_below[part, cols + LANES :])[:EDGE, :]


def shifted(x, by, axis):
    return pltpu.roll(x, by % x.shape[axis], axis)


def weights_kernel(where_ref, initial_ref, transmit_ref, land_ref, left_ref, right_ref, above_ref, below_ref, *rest):
    center_ref, up_ref, down_ref, wleft_ref, wright_ref, first_ref, ext_ref = rest
    rows, cols = initial_ref.shape
    height, width = ext_ref.shape
    sides = (left_ref, right_ref, above_ref, below_ref)
    i = iota((height, width), 0)
    j = iota((height, width), 1)
    inside = (i >= where_ref[0]) & (i < where_ref[1]) & (j >= where_ref[2]) & (j < where_ref[3])

    def extended(tile, at):
        assemble(ext_ref, tile, sides, at)
        return jnp.where(inside, ext_ref[...], 0.0)

    transmit = extended(transmit_ref[...], 1)
    share = extended(land_ref[...].astype(F32), 2)
    up = 0.5 * (transmit + shifted(transmit, 1, 0))
    down = 0.5 * (transmit + shifted(transmit, -1, 0))
    left = 0.5 * (transmit + shifted(transmit, 1, 1))
    right = 0.5 * (transmit + shifted(transmit, -1, 1))
    scale = share / (store_rate + (up + down + left + right))
    center_ref[...] = scale
    up, down, left, right = up * scale, down * scale, left * scale, right * scale
    up_ref[...] = up
    down_ref[...] = down
    wleft_ref[...] = left
    wright_ref[...] = right
    initial = extended(initial_ref[...], 0)
    inflow = up * shifted(initial, 1, 0) + down * shifted(initial, -1, 0)
    first_ref[...] = inflow + left * shifted(initial, 1, 1) + right * shifted(initial, -1, 1)


def weights(where, initial, transmit, land, sides):
    rows, cols = initial.shape
    ext = (rows + 2 * EDGE, cols + 2 * LANES)
    return pl.pallas_call(
        weights_kernel,
        out_shape=(jax.ShapeDtypeStruct(ext, F32),) * 6,
        in_specs=[pl.BlockSpec(memory_space=pltpu.SMEM)] + whole(7),
        out_specs=tuple(whole(6)),
        scratch_shapes=[pltpu.VMEM(ext, F32)],
        compiler_params=params(32),
        cost_estimate=cost(6),
        name="flow_weights",
    )(where, initial, transmit, land, *sides)


def relax_kernel(source_ref, left_ref, right_ref, above_ref, below_ref, *rest):
    center_ref, up_ref, down_ref, wleft_ref, wright_ref, first_ref, out_ref, ext_ref = rest
    rows, cols = source_ref.shape
    assemble(ext_ref, source_ref[...], (left_ref, right_ref, above_ref, below_ref), 0)
    forced = center_ref[...] * ext_ref[...]
    surface = forced + first_ref[...]
    for _ in range(SWEEPS - 1):
        inflow = up_ref[...] * shifted(surface, 1, 0) + down_ref[...] * shifted(surface, -1, 0)
        inflow = inflow + wleft_ref[...] * shifted(surface, 1, 1) + wright_ref[...] * shifted(surface, -1, 1)
        surface = forced + inflow
    out_ref[...] = surface[EDGE : EDGE + rows, LANES : LANES + cols]


def relax(source, sides, weight):
    rows, cols = source.shape
    ext = weight[0].shape
    return pl.pallas_call(
        relax_kernel,
        out_shape=jax.ShapeDtypeStruct((rows, cols), F32),
        in_specs=whole(11),
        out_specs=pl.BlockSpec(memory_space=pltpu.VMEM),
        scratch_shapes=[pltpu.VMEM(ext, F32)],
        compiler_params=params(32),
        cost_estimate=cost(5),
        name="lateral_relax",
    )(source, *sides, *weight)


def on_device(precip, head, trans_coef, land, dest, moisture, ksat):
    rows, cols = precip.shape
    row_count = lax.axis_size("row")
    col_count = lax.axis_size("col")
    peers = row_count * col_count
    owned, layers, _ = moisture.shape
    blocks = rows * cols // LANES
    cap = 2 * blocks // peers
    axes = ("row", "col")
    moist2 = moisture.reshape(owned * layers, LANES)
    dest_row = jnp.transpose(dest).reshape(1, blocks)

    sent, place = pack(dest_row, precip, head, land, peers, cap, owned)
    wide = (2 * cap + 1) * LANES
    got = lax.all_to_all(sent.reshape(peers, 1, wide), axes, split_axis=0, concat_axis=0, tiled=True)
    got = got.reshape(peers * (2 * cap + 1), LANES)

    alpha, beta, gamma = response(moist2, ksat, layers)
    initial, left, right, up, down, transmit = derive(head, trans_coef, land)
    sides = exchange(up, down, left, right)
    row_at, col_at = lax.axis_index("row"), lax.axis_index("col")
    where = jnp.stack(
        [
            jnp.where(row_at == 0, EDGE, 0),
            jnp.where(row_at == row_count - 1, EDGE + rows, 2 * EDGE + rows),
            jnp.where(col_at == 0, LANES, 0),
            jnp.where(col_at == col_count - 1, LANES + cols, 2 * LANES + cols),
        ]
    ).astype(jnp.int32)
    weight = weights(where, initial, transmit, land, sides)

    infil, share, answer = owner_side(got, alpha, beta, gamma, peers, cap)
    back = lax.all_to_all(answer.reshape(peers, cap, LANES), axes, split_axis=0, concat_axis=0, tiled=True)
    back = back.reshape(peers * cap, LANES)
    saturation = saturate(moist2, ksat, infil, share, layers).reshape(owned, layers, LANES)

    source, left, right = source_of(back, place, initial, peers, cap)
    sides = exchange(source[:EDGE, :], source[rows - EDGE :, :], left, right)
    surface = relax(source, sides, weight)
    return (saturation, surface)


def solution(mesh):
    tile = P("row", "col")
    return jax.shard_map(
        on_device,
        mesh=mesh,
        in_specs=(tile,) * 5 + (P(("row", "col"), None, None), P(("row", "col"), None)),
        out_specs=(P(("row", "col"), None, None), tile),
        check_vma=False,
    )
```

```python
import math

import jax
import jax.numpy as jnp
from jax import lax
from jax.experimental import pallas as pl
from jax.experimental.pallas import tpu as pltpu
from jax.sharding import PartitionSpec as P

SWEEPS = 4
LANES = 128
EDGE = 8
GROUPS = 4

layer_depth = 0.1
step_ratio = 0.1
residual_water = 0.05
pore_range = 0.4
couple_rate = 0.05
recharge_gain = 20.0
store_rate = 0.2

F32 = jnp.float32
BF16 = jnp.bfloat16
MIB = 1 << 20


def iota(shape, dim):
    return lax.broadcasted_iota(jnp.int32, shape, dim)


def params():
    return pltpu.CompilerParams(vmem_limit_bytes=56 * MIB)


def cost(us):
    return pl.CostEstimate(flops=0, bytes_accessed=int(us * 3.0e6), transcendentals=0)


def halves(x):
    high = x.astype(BF16)
    low = (x - high.astype(F32)).astype(BF16)
    return high, low


def hbm(x):
    return pltpu.with_memory_space_constraint(x, pltpu.HBM)


def vmem(x):
    return pltpu.with_memory_space_constraint(x, pltpu.VMEM)


def staged(body, name, ins, outs, scratch, us, after=(), held=(), left=(), pieces=None, in_smem=()):
    n, m, k = len(ins), len(outs), len(after)
    pieces = pieces or (1,) * m
    moved = [i for i in range(n) if i not in held and i not in in_smem]
    sent = [i for i in range(m) if i not in left]

    def kernel(*refs):
        in_at, out_at = refs[:n], refs[n + k : n + k + m]
        rest = refs[n + k + m :]
        in_ref = dict(zip(moved, rest))
        rest = rest[len(moved) :]
        out_ref = dict(enumerate(out_at)) | dict(zip(sent, rest))
        rest = rest[len(sent) :]
        in_sem, out_sem = rest[:2]
        reads = {i: pltpu.make_async_copy(in_at[i], in_ref[i], in_sem.at[i]) for i in moved}
        writes = {}
        for i in sent:
            size = outs[i].shape[0] // pieces[i]
            for p in range(pieces[i]):
                part = pl.ds(p * size, size)
                sem = out_sem.at[sum(pieces[:i]) + p]
                writes[i, p] = pltpu.make_async_copy(out_ref[i].at[part], out_at[i].at[part], sem)
        for read in reads.values():
            read.start()

        def take(i):
            if i not in moved:
                return in_at[i]
            reads[i].wait()
            return in_ref[i]

        body(take, [out_ref[i] for i in range(m)], lambda i, p=0: writes[i, p].start(), *rest[2:])
        for write in writes.values():
            write.wait()

    spaces = {**{i: pltpu.VMEM for i in held}, **{i: pltpu.SMEM for i in in_smem}}
    in_specs = [pl.BlockSpec(memory_space=spaces.get(i, pltpu.HBM)) for i in range(n)]
    placed = [x if i in in_smem else vmem(x) if i in held else hbm(x) for i, x in enumerate(ins)]
    return pl.pallas_call(
        kernel,
        out_shape=tuple(
            pltpu.VMEM(x.shape, x.dtype) if i in left else pltpu.HBM(x.shape, x.dtype) for i, x in enumerate(outs)
        ),
        in_specs=in_specs + [pl.BlockSpec(memory_space=pltpu.HBM)] * k,
        out_specs=tuple(pl.BlockSpec(memory_space=pltpu.VMEM if i in left else pltpu.HBM) for i in range(m)),
        scratch_shapes=[pltpu.VMEM(ins[i].shape, ins[i].dtype) for i in moved]
        + [pltpu.VMEM(outs[i].shape, outs[i].dtype) for i in sent]
        + [pltpu.SemaphoreType.DMA((n,)), pltpu.SemaphoreType.DMA((sum(pieces),))]
        + list(scratch),
        compiler_params=pltpu.CompilerParams(vmem_limit_bytes=40 * MIB),
        cost_estimate=cost(us),
        name=name,
    )(*placed, *[hbm(x) for x in after])


def floats(*shape):
    return jax.ShapeDtypeStruct(shape, F32)


def pack_kernel(peers, cap, owned, rows, cols, take, outs, give, hot_ref, data_ref):
    out_ref, place_ref = outs
    parts = cols // LANES
    blocks = rows * parts
    stride = 2 * cap + 1
    dest_ref = take(0)
    dest = jnp.concatenate([dest_ref[k : k + 1, :] for k in range(parts)], axis=1)
    shift = owned.bit_length() - 1
    owner = dest >> shift
    label = (dest & (owned - 1)) + 1
    owner_hot = owner == iota((peers, blocks), 0)
    before = (iota((LANES, LANES), 0) < iota((LANES, LANES), 1)).astype(F32).astype(BF16)
    carry = jnp.zeros((peers, 1), F32)
    ranks = []
    for chunk in range(blocks // LANES):
        hot = owner_hot[:, chunk * LANES : (chunk + 1) * LANES]
        hot_f = hot.astype(F32)
        count = jnp.dot(hot_f.astype(BF16), before, preferred_element_type=F32) + carry
        ranks.append(jnp.sum(count * hot_f, axis=0, keepdims=True))
        carry = carry + jnp.sum(hot_f, axis=1, keepdims=True)
    rank = jnp.concatenate(ranks, axis=1).astype(jnp.int32)
    place = owner + peers * rank
    place_f = place.astype(F32)
    eye = iota((LANES, LANES), 0) == iota((LANES, LANES), 1)
    for chunk in range(blocks // LANES):
        line = place_f[:, chunk * LANES : (chunk + 1) * LANES]
        place_ref[chunk * LANES : (chunk + 1) * LANES, :] = jnp.sum(
            jnp.where(eye, line, 0.0), axis=1, keepdims=True
        ).astype(jnp.int32)
    give(1)
    precip_ref, head_ref, land_ref = take(1), take(2), take(3)
    for part in range(parts):
        lane = slice(part * LANES, (part + 1) * LANES)
        line = slice(part * rows, (part + 1) * rows)
        infil = precip_ref[:, lane] * land_ref[:, lane].astype(F32)
        for at, piece in enumerate(halves(infil) + halves(head_ref[:, lane])):
            data_ref[line, at * LANES : (at + 1) * LANES] = piece
    owner_f = owner_hot.astype(F32)
    rank_hot = (rank == iota((LANES, blocks), 0)).astype(F32).astype(BF16)
    contract = (((1,), (1,)), ((), ()))
    tops = (owner_f * (label >> 5).astype(F32)).astype(BF16)
    lows = (owner_f * (label & 31).astype(F32)).astype(BF16)
    labels = 32.0 * lax.dot_general(tops, rank_hot, contract, preferred_element_type=F32)
    labels = labels + lax.dot_general(lows, rank_hot, contract, preferred_element_type=F32)
    out_ref[pl.ds(2 * cap, peers, stride=stride), :] = labels
    size = peers // GROUPS
    for group in range(GROUPS):
        for k in range(cap):
            at = (group * cap + k) * size
            hot_ref[at : at + size, :] = (
                (place == iota((size, blocks), 0) + (k * peers + group * size)).astype(F32).astype(BF16)
            )
        line = slice(group * cap * size, (group + 1) * cap * size)
        moved = jnp.dot(hot_ref[line, :], data_ref[...], preferred_element_type=F32)
        for k in range(cap):
            part = moved[k * size : (k + 1) * size]
            row = group * size * stride + k
            out_ref[pl.ds(row, size, stride=stride), :] = part[:, :LANES] + part[:, LANES : 2 * LANES]
            out_ref[pl.ds(row + cap, size, stride=stride), :] = part[:, 2 * LANES : 3 * LANES] + part[:, 3 * LANES :]
        give(0, group)


def pack(dest, precip, head, land, peers, cap, owned):
    rows, cols = precip.shape
    blocks = rows * cols // LANES

    def body(*refs):
        pack_kernel(peers, cap, owned, rows, cols, *refs)

    return staged(
        body,
        "pack_forcing",
        (jnp.transpose(dest), precip, head, land),
        (floats(peers * (2 * cap + 1), LANES), jax.ShapeDtypeStruct((blocks, 1), jnp.int32)),
        [pltpu.VMEM((peers * cap, blocks), BF16), pltpu.VMEM((blocks, 4 * LANES), BF16)],
        5,
        pieces=(GROUPS, 1),
    )


def layer_terms(moist, half_k, depth_factor):
    wet = moist * (1.0 / pore_range) - residual_water / pore_range
    wet2 = wet * wet
    a = half_k * depth_factor
    t = a * wet2
    return wet, 7.5 * t, t * wet, a + 5.0 * t


def inverse(x):
    y = pl.reciprocal(x, approx=True)
    return y * (2.0 - x * y)


def eliminate(layers, load, ksat, infil, response, keep):
    half_k = 0.5 * ksat
    moist = load(0)
    wet, hs, hc, d5 = layer_terms(moist, half_k, math.exp(-0.5 * layer_depth))
    flux_above = infil
    ratio = reduced = resp = hs_prev = g_prev = None
    for k in range(layers):
        last = k == layers - 1
        if not last:
            moist_n = load(k + 1)
            wet_n, hs_n, hc_n, d5_n = layer_terms(
                moist_n, half_k, math.exp(-(k + 1.5) * layer_depth)
            )
            g = d5 + d5_n
            flux = (hc + hc_n) - g * (moist_n - moist)
        if k == 0:
            diagonal = (g + step_ratio) + hs
        elif last:
            diagonal = (g_prev + (step_ratio + couple_rate)) + hs
        else:
            diagonal = (g_prev + step_ratio) + g
        if last:
            bottom = 2.0 * hc + couple_rate * (moist - residual_water)
            right = flux_above - bottom
        else:
            right = (0.0 - flux) if flux_above is None else (flux_above - flux)
        if k == 0:
            inv = inverse(diagonal)
            reduced = right * inv
            resp = inv
        else:
            neg_sub = hs_prev + g_prev
            inv = inverse(diagonal + neg_sub * ratio)
            reduced = (right + neg_sub * reduced) * inv
            if response:
                resp = neg_sub * resp * inv
        if last:
            return bottom, 2.0 * hs + couple_rate, reduced, resp, inv, wet
        ratio = (hs_n - g) * inv
        if keep is not None:
            keep(k, wet, ratio, reduced)
        hs_prev, g_prev = hs, g
        flux_above = flux
        moist, wet, hs, hc, d5 = moist_n, wet_n, hs_n, hc_n, d5_n


def response_kernel(layers, chunk, moist_ref, ksat_ref, alpha_ref, beta_ref, gamma_ref):
    def step(j, carry):
        base = j * (chunk * layers)
        line = pl.ds(j * chunk, chunk)
        load = lambda k: moist_ref[pl.ds(base + k, chunk, stride=layers), :]
        bottom, gain, reduced, resp, inv, _ = eliminate(layers, load, ksat_ref[line, :], None, True, None)
        alpha_ref[line, :] = bottom + gain * reduced
        beta_ref[line, :] = gain * resp
        gamma_ref[line, :] = (couple_rate * pore_range) * (gain * inv - 1.0)
        return carry

    lax.fori_loop(0, ksat_ref.shape[0] // chunk, step, 0)


def response(moist2, ksat, layers, half, count, after=()):
    owned = ksat.shape[0] // count
    size = 128
    first = half * (owned // size)

    def kernel(moist_ref, ksat_ref, *refs):
        response_kernel(layers, 32, moist_ref, ksat_ref, *refs[len(after) :])

    small = pl.BlockSpec((size, LANES), lambda i: (i, 0))
    return pl.pallas_call(
        kernel,
        grid=(owned // size,),
        out_shape=(pltpu.HBM((owned, LANES), F32),) * 3,
        in_specs=[
            pl.BlockSpec((size * layers, LANES), lambda i: (i + first, 0)),
            pl.BlockSpec((size, LANES), lambda i: (i + first, 0)),
        ]
        + [pl.BlockSpec(memory_space=pltpu.HBM)] * len(after),
        out_specs=(small,) * 3,
        compiler_params=params(),
        cost_estimate=cost(13 / count),
        name="column_response",
    )(*[hbm(x) for x in (moist2, ksat, *after)])


def saturation_kernel(layers, chunk, moist_ref, ksat_ref, infil_ref, share_ref, out_ref, wet_s, ratio_s, reduced_s):
    def step(j, carry):
        base = j * (chunk * layers)
        line = pl.ds(j * chunk, chunk)
        load = lambda k: moist_ref[pl.ds(base + k, chunk, stride=layers), :]

        def keep(k, wet, ratio, reduced):
            wet_s[k] = wet
            ratio_s[k] = ratio
            reduced_s[k] = reduced

        _, _, reduced, _, inv, wet = eliminate(layers, load, ksat_ref[line, :], infil_ref[line, :], False, keep)
        change = reduced + (couple_rate * pore_range) * share_ref[line, :] * inv
        out_ref[pl.ds(base + layers - 1, chunk, stride=layers), :] = wet + (1.0 / pore_range) * change
        for k in range(layers - 2, -1, -1):
            change = reduced_s[k] - ratio_s[k] * change
            out_ref[pl.ds(base + k, chunk, stride=layers), :] = wet_s[k] + (1.0 / pore_range) * change
        return carry

    lax.fori_loop(0, ksat_ref.shape[0] // chunk, step, 0)


def saturate(moist2, ksat, infil, share, layers):
    owned = ksat.shape[0]
    size, chunk = 128, 32

    def kernel(*refs):
        saturation_kernel(layers, chunk, *refs)

    small = pl.BlockSpec((size, LANES), lambda i: (i, 0))
    large = pl.BlockSpec((size * layers, LANES), lambda i: (i, 0))
    return pl.pallas_call(
        kernel,
        grid=(owned // size,),
        out_shape=pltpu.HBM((owned * layers, LANES), F32),
        in_specs=[large, small, small, small],
        out_specs=large,
        scratch_shapes=[pltpu.VMEM((layers - 1, chunk, LANES), F32)] * 3,
        compiler_params=params(),
        cost_estimate=cost(14),
        name="column_saturation",
    )(*[hbm(x) for x in (moist2, ksat, infil, share)])


def owner_kernel(peers, cap, owned, take, outs, give, data_ref, hot_ref, back_ref, rech_ref):
    infil_ref, share_ref, ans_ref = outs
    got_ref = take(0)
    stride = 2 * cap + 1
    labels = got_ref[pl.ds(2 * cap, peers, stride=stride), :]
    turned = jnp.transpose(labels).astype(jnp.int32) - 1
    labels = labels.astype(jnp.int32) - 1
    for k in range(cap):
        line = slice(k * peers, (k + 1) * peers)
        pieces = halves(got_ref[pl.ds(k, peers, stride=stride), :])
        pieces = pieces + halves(got_ref[pl.ds(cap + k, peers, stride=stride), :])
        for at, piece in enumerate(pieces):
            data_ref[line, at * LANES : (at + 1) * LANES] = piece
        hot_ref[:, line] = (turned[k : k + 1, :] == iota((owned, peers), 0)).astype(F32).astype(BF16)
    responses = [take(1 + k) for k in range(3)]
    group = 512
    alpha_ref, beta_ref, gamma_ref = responses
    for first in range(0, owned, group):
        line = slice(first, first + group)
        moved = jnp.dot(hot_ref[line, :], data_ref[...], preferred_element_type=F32)
        infil = moved[:, :LANES] + moved[:, LANES : 2 * LANES]
        head = moved[:, 2 * LANES : 3 * LANES] + moved[:, 3 * LANES :]
        share = jax.nn.sigmoid(head)
        infil_ref[line, :] = infil
        share_ref[line, :] = share
        rech = alpha_ref[line, :] + beta_ref[line, :] * infil + gamma_ref[line, :] * share
        high, low = halves(rech)
        rech_ref[line, :LANES] = high
        rech_ref[line, LANES:] = low
    give(0)
    give(1)
    size = peers // GROUPS
    for first in range(0, peers, size):
        for k in range(cap):
            at = first * cap + k * size
            back_ref[at : at + size, :] = (
                (labels[first : first + size, k : k + 1] == iota((size, owned), 1)).astype(F32).astype(BF16)
            )
        line = slice(first * cap, (first + size) * cap)
        moved = jnp.dot(back_ref[line, :], rech_ref[...], preferred_element_type=F32)
        for k in range(cap):
            part = moved[k * size : (k + 1) * size]
            ans_ref[pl.ds(first * cap + k, size, stride=cap), :] = part[:, :LANES] + part[:, LANES:]
        give(2, first // size)


def owner_side(got, responses, peers, cap, after):
    owned = responses[0].shape[0]

    def body(*refs):
        owner_kernel(peers, cap, owned, *refs)

    return staged(
        body,
        "owner_side",
        (got,) + tuple(responses),
        (floats(owned, LANES), floats(owned, LANES), floats(peers * cap, LANES)),
        [
            pltpu.VMEM((peers * cap, 4 * LANES), BF16),
            pltpu.VMEM((owned, peers * cap), BF16),
            pltpu.VMEM((peers * cap, owned), BF16),
            pltpu.VMEM((owned, 2 * LANES), BF16),
        ],
        8,
        after,
        held=(0,),
        pieces=(1, 1, GROUPS),
    )


def put_sides(x, left_ref, right_ref, at):
    cols = x.shape[1]
    left_ref[at : at + EDGE, :] = jnp.transpose(x[:, :LANES])[:EDGE, :]
    right_ref[at : at + EDGE, :] = jnp.transpose(x[:, cols - LANES :])[LANES - EDGE :, :]


def source_kernel(peers, cap, take, outs, give, data_ref, hot_ref):
    source_ref, left_ref, right_ref, up_ref, down_ref = outs
    rows, cols = source_ref.shape
    blocks = rows * cols // LANES
    place = take(1)[...]
    for k in range(cap):
        line = slice(k * peers, (k + 1) * peers)
        hot_ref[:, line] = (place == iota((blocks, peers), 1) + k * peers).astype(F32).astype(BF16)
    back_ref = take(0)
    for k in range(cap):
        line = slice(k * peers, (k + 1) * peers)
        high, low = halves(back_ref[pl.ds(k, peers, stride=cap), :])
        data_ref[line, :LANES] = high
        data_ref[line, LANES:] = low
    initial_ref = take(2)
    for part in range(cols // LANES):
        lane = slice(part * LANES, (part + 1) * LANES)
        moved = jnp.dot(hot_ref[part * rows : (part + 1) * rows, :], data_ref[...], preferred_element_type=F32)
        source_ref[:, lane] = store_rate * initial_ref[:, lane] + recharge_gain * (
            moved[:, :LANES] + moved[:, LANES:]
        )
    put_sides(source_ref[...], left_ref, right_ref, 0)
    up_ref[:EDGE, :] = source_ref[:EDGE, :]
    down_ref[:EDGE, :] = source_ref[rows - EDGE :, :]
    for i, ref in enumerate((left_ref, right_ref, up_ref, down_ref)):
        ref[EDGE:, :] = take(3 + i)[...]


def source_of(back, place, initial, edges, peers, cap, after):
    rows, cols = initial.shape
    blocks = place.shape[0]
    side, line = floats(4 * EDGE, rows), floats(4 * EDGE, cols)

    def body(*refs):
        source_kernel(peers, cap, *refs)

    return staged(
        body,
        "tile_source",
        (back, place, initial) + tuple(edges),
        (floats(rows, cols), side, side, line, line),
        [pltpu.VMEM((peers * cap, 2 * LANES), BF16), pltpu.VMEM((blocks, peers * cap), BF16)],
        4,
        after,
        held=(0,),
        left=range(5),
    )


def derive_kernel(take, outs, give):
    initial_ref, left_ref, right_ref, up_ref, down_ref, transmit_ref = outs
    rows = initial_ref.shape[0]
    head = take(0)[...]
    share = take(2)[...].astype(F32)
    initial = head * share
    initial_ref[...] = initial
    transmit = take(1)[...] * (1.0 + 0.5 * jnp.tanh(head))
    transmit_ref[...] = transmit
    for at, x in enumerate((initial, transmit, share)):
        put_sides(x, left_ref, right_ref, at * EDGE)
        up_ref[at * EDGE : (at + 1) * EDGE, :] = x[:EDGE, :]
        down_ref[at * EDGE : (at + 1) * EDGE, :] = x[rows - EDGE :, :]
    for i in range(6):
        give(i)


def derive(head, trans_coef, land):
    rows, cols = head.shape
    tile, side, line = floats(rows, cols), floats(3 * EDGE, rows), floats(3 * EDGE, cols)
    return staged(
        derive_kernel, "derive_tile", (head, trans_coef, land), (tile, side, side, line, line, tile), [], 3
    )


def exchange(up_line, down_line, left_side, right_side):
    rows = left_side.shape[1]

    def ring(axis, by):
        count = lax.axis_size(axis)
        return [(i, (i + by) % count) for i in range(count)]

    from_left = lax.ppermute(right_side, "col", ring("col", 1))
    from_right = lax.ppermute(left_side, "col", ring("col", -1))
    down_send = jnp.concatenate([down_line, from_left[:, rows - LANES :], from_right[:, rows - LANES :]], axis=1)
    up_send = jnp.concatenate([up_line, from_left[:, :LANES], from_right[:, :LANES]], axis=1)
    from_above = lax.ppermute(down_send, "row", ring("row", 1))
    from_below = lax.ppermute(up_send, "row", ring("row", -1))
    return from_left, from_right, from_above, from_below


def left_block(side):
    return jnp.transpose(jnp.concatenate([jnp.zeros((LANES - EDGE, LANES), F32), side], axis=0))


def right_block(side):
    return jnp.transpose(jnp.concatenate([side, jnp.zeros((LANES - EDGE, LANES), F32)], axis=0))


def put_edges(out_ref, rows, cols, sides, at):
    from_left, from_right, from_above, from_below = sides
    part = slice(at * EDGE, (at + 1) * EDGE)
    bottom = slice(EDGE + rows, 2 * EDGE + rows)
    right = slice(LANES + cols, 2 * LANES + cols)
    mid = slice(LANES, LANES + cols)
    out_ref[:EDGE, mid] = from_above[part, :cols]
    out_ref[bottom, mid] = from_below[part, :cols]
    for first in range(0, rows, LANES):
        line = slice(EDGE + first, EDGE + first + LANES)
        out_ref[line, :LANES] = left_block(from_left[part, first : first + LANES])
        out_ref[line, right] = right_block(from_right[part, first : first + LANES])
    out_ref[:EDGE, :LANES] = left_block(from_above[part, cols : cols + LANES])[LANES - EDGE :, :]
    out_ref[:EDGE, right] = right_block(from_above[part, cols + LANES :])[LANES - EDGE :, :]
    out_ref[bottom, :LANES] = left_block(from_below[part, cols : cols + LANES])[:EDGE, :]
    out_ref[bottom, right] = right_block(from_below[part, cols + LANES :])[:EDGE, :]


def shifted(x, by, axis):
    return pltpu.roll(x, by % x.shape[axis], axis)


def relax_kernel(take, outs, give, *ext_refs):
    (out_ref,) = outs
    rows, cols = out_ref.shape
    height, width = ext_refs[0].shape
    where = take(0)
    sides = [take(5 + i) for i in range(4)]
    for at in range(4):
        put_edges(ext_refs[at], rows, cols, sides, at)
    i = iota((height, width), 0)
    j = iota((height, width), 1)
    inside = (i >= where[0]) & (i < where[1]) & (j >= where[2]) & (j < where[3])

    def extended(tile, at):
        ext_refs[at][EDGE : EDGE + rows, LANES : LANES + cols] = tile
        return jnp.where(inside, ext_refs[at][...], 0.0)

    transmit = extended(take(1)[...], 2)
    share = extended(take(2)[...].astype(F32), 3)
    up = 0.5 * (transmit + shifted(transmit, 1, 0))
    down = 0.5 * (transmit + shifted(transmit, -1, 0))
    left = 0.5 * (transmit + shifted(transmit, 1, 1))
    right = 0.5 * (transmit + shifted(transmit, -1, 1))
    scale = share / (store_rate + (up + down + left + right))
    up_ref, down_ref, left_ref, right_ref = ext_refs[4:]
    up_ref[...] = up * scale
    down_ref[...] = down * scale
    left_ref[...] = left * scale
    right_ref[...] = right * scale
    surface = extended(take(3)[...], 1)
    forced = scale * extended(take(4)[...], 0)
    for _ in range(SWEEPS):
        inflow = up_ref[...] * shifted(surface, 1, 0) + down_ref[...] * shifted(surface, -1, 0)
        inflow = inflow + left_ref[...] * shifted(surface, 1, 1) + right_ref[...] * shifted(surface, -1, 1)
        surface = forced + inflow
    out_ref[...] = surface[EDGE : EDGE + rows, LANES : LANES + cols]
    give(0)


def relax(where, transmit, land, initial, source, sides):
    rows, cols = source.shape
    ext = (rows + 2 * EDGE, cols + 2 * LANES)
    return staged(
        relax_kernel,
        "lateral_relax",
        (where, transmit, land, initial, source) + tuple(sides),
        (floats(rows, cols),),
        [pltpu.VMEM(ext, F32)] * 8,
        6,
        held=range(4, 9),
        in_smem=(0,),
    )[0]


def on_device(precip, head, trans_coef, land, dest, moisture, ksat):
    rows, cols = precip.shape
    row_count = lax.axis_size("row")
    col_count = lax.axis_size("col")
    peers = row_count * col_count
    owned, layers, _ = moisture.shape
    cap = 2 * (rows * cols // LANES) // peers
    axes = ("row", "col")
    moist2 = moisture.reshape(owned * layers, LANES)

    sent, place = pack(dest, precip, head, land, peers, cap, owned)
    wide = (2 * cap + 1) * LANES
    got = lax.all_to_all(sent.reshape(peers, 1, wide), axes, split_axis=0, concat_axis=0, tiled=True)
    got = got.reshape(peers * (2 * cap + 1), LANES)

    initial, left, right, up, down, transmit = derive(head, trans_coef, land)
    responses = response(moist2, ksat, layers, 0, 1, (left,))
    row_at, col_at = lax.axis_index("row"), lax.axis_index("col")
    where = jnp.stack(
        [
            jnp.where(row_at == 0, EDGE, 0),
            jnp.where(row_at == row_count - 1, EDGE + rows, 2 * EDGE + rows),
            jnp.where(col_at == 0, LANES, 0),
            jnp.where(col_at == col_count - 1, LANES + cols, 2 * LANES + cols),
        ]
    ).astype(jnp.int32)

    infil, share, answer = owner_side(got, responses, peers, cap, ())
    back = lax.all_to_all(answer.reshape(peers, cap, LANES), axes, split_axis=0, concat_axis=0, tiled=True)
    back = back.reshape(peers * cap, LANES)
    saturation = saturate(moist2, ksat, infil, share, layers)

    source, *edges = source_of(back, place, initial, (left, right, up, down), peers, cap, (saturation,))
    left, right, up, down = edges
    surface = relax(where, transmit, land, initial, source, exchange(up, down, left, right))
    return (saturation.reshape(owned, layers, LANES), surface)


def solution(mesh):
    tile = P("row", "col")
    return jax.shard_map(
        on_device,
        mesh=mesh,
        in_specs=(tile,) * 5 + (P(("row", "col"), None, None), P(("row", "col"), None)),
        out_specs=(P(("row", "col"), None, None), tile),
        check_vma=False,
    )
```

```python
import math

import jax
import jax.numpy as jnp
from jax import lax
from jax.experimental import pallas as pl
from jax.experimental.pallas import tpu as pltpu
from jax.sharding import PartitionSpec as P

SWEEPS = 4
LANES = 128
EDGE = 8
PAD = 8
GROUPS = 4

layer_depth = 0.1
step_ratio = 0.1
residual_water = 0.05
pore_range = 0.4
couple_rate = 0.05
recharge_gain = 20.0
store_rate = 0.2

F32 = jnp.float32
BF16 = jnp.bfloat16
MIB = 1 << 20


def iota(shape, dim):
    return lax.broadcasted_iota(jnp.int32, shape, dim)


def params():
    return pltpu.CompilerParams(vmem_limit_bytes=24 * MIB)


def cost(us):
    return pl.CostEstimate(flops=0, bytes_accessed=int(us * 3.0e6), transcendentals=0)


def halves(x):
    high = x.astype(BF16)
    low = (x - high.astype(F32)).astype(BF16)
    return high, low


def hbm(x):
    return pltpu.with_memory_space_constraint(x, pltpu.HBM)


def vmem(x):
    return pltpu.with_memory_space_constraint(x, pltpu.VMEM)


def staged(body, name, ins, outs, scratch, us, after=(), held=(), left=(), pieces=None, by_lanes=False, in_smem=(), small=False):
    n, m, k = len(ins), len(outs), len(after)
    pieces = pieces or (1,) * m
    moved = [i for i in range(n) if i not in held and i not in in_smem]
    sent = [i for i in range(m) if i not in left]

    def kernel(*refs):
        in_at, out_at = refs[:n], refs[n + k : n + k + m]
        rest = refs[n + k + m :]
        in_ref = dict(zip(moved, rest))
        rest = rest[len(moved) :]
        out_ref = dict(enumerate(out_at)) | dict(zip(sent, rest))
        rest = rest[len(sent) :]
        in_sem, out_sem = rest[:2]
        reads = {i: pltpu.make_async_copy(in_at[i], in_ref[i], in_sem.at[i]) for i in moved}
        writes = {}
        for i in sent:
            size = outs[i].shape[by_lanes] // pieces[i]
            for p in range(pieces[i]):
                part = pl.ds(p * size, size)
                part = (slice(None), part) if by_lanes else part
                sem = out_sem.at[sum(pieces[:i]) + p]
                writes[i, p] = pltpu.make_async_copy(out_ref[i].at[part], out_at[i].at[part], sem)
        for read in reads.values():
            read.start()

        def take(i):
            if i not in moved:
                return in_at[i]
            reads[i].wait()
            return in_ref[i]

        body(take, [out_ref[i] for i in range(m)], lambda i, p=0: writes[i, p].start(), *rest[2:])
        for write in writes.values():
            write.wait()

    spaces = {**{i: pltpu.VMEM for i in held}, **{i: pltpu.SMEM for i in in_smem}}
    in_specs = [pl.BlockSpec(memory_space=spaces.get(i, pltpu.HBM)) for i in range(n)]
    placed = [x if i in in_smem else vmem(x) if i in held else hbm(x) for i, x in enumerate(ins)]
    return pl.pallas_call(
        kernel,
        out_shape=tuple(
            pltpu.VMEM(x.shape, x.dtype) if i in left else pltpu.HBM(x.shape, x.dtype) for i, x in enumerate(outs)
        ),
        in_specs=in_specs + [pl.BlockSpec(memory_space=pltpu.VMEM if small else pltpu.HBM)] * k,
        out_specs=tuple(pl.BlockSpec(memory_space=pltpu.VMEM if i in left else pltpu.HBM) for i in range(m)),
        scratch_shapes=[pltpu.VMEM(ins[i].shape, ins[i].dtype) for i in moved]
        + [pltpu.VMEM(outs[i].shape, outs[i].dtype) for i in sent]
        + [pltpu.SemaphoreType.DMA((n,)), pltpu.SemaphoreType.DMA((sum(pieces),))]
        + list(scratch),
        compiler_params=pltpu.CompilerParams(vmem_limit_bytes=40 * MIB),
        cost_estimate=cost(us),
        name=name,
    )(*placed, *[vmem(x) if small else hbm(x) for x in after])


def floats(*shape):
    return jax.ShapeDtypeStruct(shape, F32)


def pack_kernel(peers, cap, owned, rows, cols, take, outs, give, hot_ref, data_ref):
    out_ref, place_ref = outs
    parts = cols // LANES
    blocks = rows * parts
    stride = 2 * cap + 1
    dest_ref = take(0)
    dest = jnp.concatenate([dest_ref[k : k + 1, :] for k in range(parts)], axis=1)
    shift = owned.bit_length() - 1
    owner = dest >> shift
    label = (dest & (owned - 1)) + 1
    owner_hot = owner == iota((peers, blocks), 0)
    before = (iota((LANES, LANES), 0) < iota((LANES, LANES), 1)).astype(F32).astype(BF16)
    carry = jnp.zeros((peers, 1), F32)
    ranks = []
    for chunk in range(blocks // LANES):
        hot = owner_hot[:, chunk * LANES : (chunk + 1) * LANES]
        hot_f = hot.astype(F32)
        count = jnp.dot(hot_f.astype(BF16), before, preferred_element_type=F32) + carry
        ranks.append(jnp.sum(count * hot_f, axis=0, keepdims=True))
        carry = carry + jnp.sum(hot_f, axis=1, keepdims=True)
    rank = jnp.concatenate(ranks, axis=1).astype(jnp.int32)
    place = owner + peers * rank
    place_ref[...] = place
    give(1)
    owner_f = owner_hot.astype(F32)
    rank_hot = (rank == iota((LANES, blocks), 0)).astype(F32).astype(BF16)
    contract = (((1,), (1,)), ((), ()))
    tops = (owner_f * (label >> 5).astype(F32)).astype(BF16)
    lows = (owner_f * (label & 31).astype(F32)).astype(BF16)
    labels = 32.0 * lax.dot_general(tops, rank_hot, contract, preferred_element_type=F32)
    labels = labels + lax.dot_general(lows, rank_hot, contract, preferred_element_type=F32)
    out_ref[pl.ds(2 * cap, peers, stride=stride), :] = labels
    size = peers // GROUPS

    def mark(group):
        for k in range(cap):
            at = (group * cap + k) * size
            hot_ref[at : at + size, :] = (
                (place == iota((size, blocks), 0) + (k * peers + group * size)).astype(F32).astype(BF16)
            )

    mark(0)
    precip_ref, head_ref, land_ref = take(1), take(2), take(3)
    for part in range(parts):
        lane = slice(part * LANES, (part + 1) * LANES)
        line = slice(part * rows, (part + 1) * rows)
        infil = precip_ref[:, lane] * land_ref[:, lane].astype(F32)
        for at, piece in enumerate(halves(infil) + halves(head_ref[:, lane])):
            data_ref[line, at * LANES : (at + 1) * LANES] = piece
    for group in range(GROUPS):
        if group + 1 < GROUPS:
            mark(group + 1)
        line = slice(group * cap * size, (group + 1) * cap * size)
        moved = jnp.dot(hot_ref[line, :], data_ref[...], preferred_element_type=F32)
        for k in range(cap):
            part = moved[k * size : (k + 1) * size]
            row = group * size * stride + k
            out_ref[pl.ds(row, size, stride=stride), :] = part[:, :LANES] + part[:, LANES : 2 * LANES]
            out_ref[pl.ds(row + cap, size, stride=stride), :] = part[:, 2 * LANES : 3 * LANES] + part[:, 3 * LANES :]
        give(0, group)


def pack(dest, precip, head, land, peers, cap, owned):
    rows, cols = precip.shape
    blocks = rows * cols // LANES

    def body(*refs):
        pack_kernel(peers, cap, owned, rows, cols, *refs)

    return staged(
        body,
        "pack_forcing",
        (jnp.transpose(dest), precip, head, land),
        (floats(peers * (2 * cap + 1), LANES), jax.ShapeDtypeStruct((1, blocks), jnp.int32)),
        [pltpu.VMEM((peers * cap, blocks), BF16), pltpu.VMEM((blocks, 4 * LANES), BF16)],
        5,
        pieces=(GROUPS, 1),
    )


def layer_terms(moist, half_k, depth_factor):
    wet = moist * (1.0 / pore_range) - residual_water / pore_range
    wet2 = wet * wet
    a = half_k * depth_factor
    t = a * wet2
    return wet, 7.5 * t, t * wet, a + 5.0 * t


def inverse(x):
    return 1.0 / x


def eliminate(layers, load, ksat, infil, response, keep):
    half_k = 0.5 * ksat
    moist = load(0)
    wet, hs, hc, d5 = layer_terms(moist, half_k, math.exp(-0.5 * layer_depth))
    flux_above = infil
    ratio = reduced = resp = hs_prev = g_prev = None
    for k in range(layers):
        last = k == layers - 1
        if not last:
            moist_n = load(k + 1)
            wet_n, hs_n, hc_n, d5_n = layer_terms(
                moist_n, half_k, math.exp(-(k + 1.5) * layer_depth)
            )
            g = d5 + d5_n
            flux = (hc + hc_n) - g * (moist_n - moist)
        if k == 0:
            diagonal = (g + step_ratio) + hs
        elif last:
            diagonal = (g_prev + (step_ratio + couple_rate)) + hs
        else:
            diagonal = (g_prev + step_ratio) + g
        if last:
            bottom = 2.0 * hc + couple_rate * (moist - residual_water)
            right = flux_above - bottom
        else:
            right = (0.0 - flux) if flux_above is None else (flux_above - flux)
        if k == 0:
            inv = inverse(diagonal)
            reduced = right * inv
            resp = inv
        else:
            neg_sub = hs_prev + g_prev
            inv = inverse(diagonal + neg_sub * ratio)
            reduced = (right + neg_sub * reduced) * inv
            if response:
                resp = neg_sub * resp * inv
        if last:
            return bottom, 2.0 * hs + couple_rate, reduced, resp, inv, wet
        ratio = (hs_n - g) * inv
        if keep is not None:
            keep(k, wet, ratio, reduced)
        hs_prev, g_prev = hs, g
        flux_above = flux
        moist, wet, hs, hc, d5 = moist_n, wet_n, hs_n, hc_n, d5_n


def response_kernel(layers, chunk, moist_ref, ksat_ref, alpha_ref, beta_ref, gamma_ref):
    def step(j, carry):
        base = j * (chunk * layers)
        line = pl.ds(j * chunk, chunk)
        load = lambda k: moist_ref[pl.ds(base + k, chunk, stride=layers), :]
        bottom, gain, reduced, resp, inv, _ = eliminate(layers, load, ksat_ref[line, :], None, True, None)
        alpha_ref[line, :] = bottom + gain * reduced
        beta_ref[line, :] = gain * resp
        gamma_ref[line, :] = (couple_rate * pore_range) * (gain * inv - 1.0)
        return carry

    lax.fori_loop(0, ksat_ref.shape[0] // chunk, step, 0)


def response(moist2, ksat, layers):
    owned = ksat.shape[0]
    size = 128

    def kernel(*refs):
        response_kernel(layers, 128, *refs)

    small = pl.BlockSpec((size, LANES), lambda i: (i, 0))
    return pl.pallas_call(
        kernel,
        grid=(owned // size,),
        out_shape=(pltpu.HBM((owned, LANES), F32),) * 3,
        in_specs=[pl.BlockSpec((size * layers, LANES), lambda i: (i, 0)), small],
        out_specs=(small,) * 3,
        compiler_params=params(),
        cost_estimate=cost(13),
        name="column_response",
    )(hbm(moist2), hbm(ksat))


def saturation_kernel(layers, chunk, moist_ref, ksat_ref, infil_ref, share_ref, out_ref, wet_s, ratio_s, reduced_s):
    def step(j, carry):
        base = j * (chunk * layers)
        line = pl.ds(j * chunk, chunk)
        load = lambda k: moist_ref[pl.ds(base + k, chunk, stride=layers), :]

        def keep(k, wet, ratio, reduced):
            wet_s[k] = wet
            ratio_s[k] = ratio
            reduced_s[k] = reduced

        _, _, reduced, _, inv, wet = eliminate(layers, load, ksat_ref[line, :], infil_ref[line, :], False, keep)
        change = reduced + (couple_rate * pore_range) * share_ref[line, :] * inv
        out_ref[pl.ds(base + layers - 1, chunk, stride=layers), :] = wet + (1.0 / pore_range) * change
        for k in range(layers - 2, -1, -1):
            change = reduced_s[k] - ratio_s[k] * change
            out_ref[pl.ds(base + k, chunk, stride=layers), :] = wet_s[k] + (1.0 / pore_range) * change
        return carry

    lax.fori_loop(0, ksat_ref.shape[0] // chunk, step, 0)


def saturate(moist2, ksat, infil, share, layers):
    owned = ksat.shape[0]
    size, chunk = 128, 32

    def kernel(*refs):
        saturation_kernel(layers, chunk, *refs)

    small = pl.BlockSpec((size, LANES), lambda i: (i, 0))
    large = pl.BlockSpec((size * layers, LANES), lambda i: (i, 0))
    return pl.pallas_call(
        kernel,
        grid=(owned // size,),
        out_shape=pltpu.HBM((owned * layers, LANES), F32),
        in_specs=[large, small, small, small],
        out_specs=large,
        scratch_shapes=[pltpu.VMEM((layers - 1, chunk, LANES), F32)] * 3,
        compiler_params=params(),
        cost_estimate=cost(14),
        name="column_saturation",
    )(*[hbm(x) for x in (moist2, ksat, infil, share)])


def owner_kernel(peers, cap, owned, take, outs, give, data_ref, hot_ref, back_ref, rech_ref):
    infil_ref, share_ref, ans_ref = outs
    got_ref = take(0)
    stride = 2 * cap + 1
    labels = got_ref[pl.ds(2 * cap, peers, stride=stride), :]
    turned = jnp.transpose(labels).astype(jnp.int32) - 1
    labels = labels.astype(jnp.int32) - 1
    group = owned // 2

    def mark(first):
        for k in range(cap):
            hot_ref[first : first + group, k * peers : (k + 1) * peers] = (
                (turned[k : k + 1, :] == iota((group, peers), 0) + first).astype(F32).astype(BF16)
            )

    for k in range(cap):
        line = slice(k * peers, (k + 1) * peers)
        pieces = halves(got_ref[pl.ds(k, peers, stride=stride), :])
        pieces = pieces + halves(got_ref[pl.ds(cap + k, peers, stride=stride), :])
        for at, piece in enumerate(pieces):
            data_ref[line, at * LANES : (at + 1) * LANES] = piece
    mark(0)
    alpha_ref, beta_ref, gamma_ref = [take(1 + k) for k in range(3)]
    mark(group)
    for first in range(0, owned, group):
        line = slice(first, first + group)
        moved = jnp.dot(hot_ref[line, :], data_ref[...], preferred_element_type=F32)
        infil = moved[:, :LANES] + moved[:, LANES : 2 * LANES]
        head = moved[:, 2 * LANES : 3 * LANES] + moved[:, 3 * LANES :]
        share = jax.nn.sigmoid(head)
        infil_ref[line, :] = infil
        share_ref[line, :] = share
        rech = alpha_ref[line, :] + beta_ref[line, :] * infil + gamma_ref[line, :] * share
        high, low = halves(rech)
        rech_ref[line, :LANES] = high
        rech_ref[line, LANES:] = low
    size = peers // GROUPS
    for turn in range(GROUPS):
        first = turn * size
        for k in range(cap):
            at = first * cap + k * size
            back_ref[at : at + size, :] = (
                (labels[first : first + size, k : k + 1] == iota((size, owned), 1)).astype(F32).astype(BF16)
            )
    for turn in range(GROUPS):
        first = turn * size
        line = slice(first * cap, (first + size) * cap)
        moved = jnp.dot(back_ref[line, :], rech_ref[...], preferred_element_type=F32)
        for k in range(cap):
            part = moved[k * size : (k + 1) * size]
            ans_ref[pl.ds(first * cap + k, size, stride=cap), :] = part[:, :LANES] + part[:, LANES:]
        if turn == 1:
            give(0)
            give(1)
            give(2, 0)
        if turn > 0:
            give(2, turn)


def owner_side(got, responses, peers, cap, after):
    owned = responses[0].shape[0]

    def body(*refs):
        owner_kernel(peers, cap, owned, *refs)

    return staged(
        body,
        "owner_side",
        (got,) + tuple(responses),
        (floats(owned, LANES), floats(owned, LANES), floats(peers * cap, LANES)),
        [
            pltpu.VMEM((peers * cap, 4 * LANES), BF16),
            pltpu.VMEM((owned, peers * cap), BF16),
            pltpu.VMEM((peers * cap, owned), BF16),
            pltpu.VMEM((owned, 2 * LANES), BF16),
        ],
        8,
        after,
        held=(0,),
        pieces=(1, 1, GROUPS),
        small=True,
    )


def put_sides(x, left_ref, right_ref, at):
    cols = x.shape[1]
    left_ref[at : at + EDGE, :] = jnp.transpose(x[:, :LANES])[:EDGE, :]
    right_ref[at : at + EDGE, :] = jnp.transpose(x[:, cols - LANES :])[LANES - EDGE :, :]


def source_kernel(peers, cap, take, outs, give, data_ref, hot_ref):
    flow_ref, left_ref, right_ref, up_ref, down_ref = outs
    rows, cols = flow_ref.shape
    blocks = rows * cols // LANES
    back_ref = take(0)
    for k in range(cap):
        line = slice(k * peers, (k + 1) * peers)
        high, low = halves(back_ref[pl.ds(k, peers, stride=cap), :])
        data_ref[line, :LANES] = high
        data_ref[line, LANES:] = low
    place_f = take(1)[...].astype(F32)
    for i, ref in enumerate((left_ref, right_ref, up_ref, down_ref)):
        ref[EDGE:, :] = take(2 + i)[...]
    eye = iota((LANES, LANES), 0) == iota((LANES, LANES), 1)
    for first in range(0, blocks, LANES):
        column = jnp.sum(jnp.where(eye, place_f[:, first : first + LANES], 0.0), axis=1, keepdims=True)
        column = column.astype(jnp.int32)
        for k in range(cap):
            hot_ref[first : first + LANES, k * peers : (k + 1) * peers] = (
                (column == iota((LANES, peers), 1) + k * peers).astype(F32).astype(BF16)
            )
    for part in range(cols // LANES):
        moved = jnp.dot(hot_ref[part * rows : (part + 1) * rows, :], data_ref[...], preferred_element_type=F32)
        flow = recharge_gain * (moved[:, :LANES] + moved[:, LANES:])
        flow_ref[:, part * LANES : (part + 1) * LANES] = flow
        if part == 0:
            left_ref[:EDGE, :] = jnp.transpose(flow)[:EDGE, :]
    right_ref[:EDGE, :] = jnp.transpose(flow)[LANES - EDGE :, :]
    up_ref[:EDGE, :] = flow_ref[:EDGE, :]
    down_ref[:EDGE, :] = flow_ref[rows - EDGE :, :]


def source_of(back, place, edges, peers, cap, after):
    rows, cols = edges[0].shape[1], edges[2].shape[1]
    blocks = place.shape[1]
    side, line = floats(4 * EDGE, rows), floats(4 * EDGE, cols)

    def body(*refs):
        source_kernel(peers, cap, *refs)

    return staged(
        body,
        "tile_source",
        (back, place) + tuple(edges),
        (floats(rows, cols), side, side, line, line),
        [pltpu.VMEM((peers * cap, 2 * LANES), BF16), pltpu.VMEM((blocks, peers * cap), BF16)],
        4,
        after,
        held=(0, 2, 3, 4, 5),
        left=range(5),
    )


def derive_kernel(take, outs, give):
    initial_ref, left_ref, right_ref, up_ref, down_ref, transmit_ref, share_ref = outs
    rows = initial_ref.shape[0]
    head = take(0)[...]
    share = take(2)[...].astype(F32)
    initial = head * share
    initial_ref[...] = initial
    share_ref[...] = share
    transmit = take(1)[...] * (1.0 + 0.5 * jnp.tanh(head))
    transmit_ref[...] = transmit
    for at, x in enumerate((initial, transmit, share)):
        put_sides(x, left_ref, right_ref, at * EDGE)
        up_ref[at * EDGE : (at + 1) * EDGE, :] = x[:EDGE, :]
        down_ref[at * EDGE : (at + 1) * EDGE, :] = x[rows - EDGE :, :]


def derive(head, trans_coef, land):
    rows, cols = head.shape
    tile, side, line = floats(rows, cols), floats(3 * EDGE, rows), floats(3 * EDGE, cols)
    return staged(
        derive_kernel,
        "derive_tile",
        (head, trans_coef, land),
        (tile, side, side, line, line, tile, tile),
        [],
        2,
        left=range(7),
    )


def exchange(up_line, down_line, left_side, right_side):
    rows = left_side.shape[1]

    def ring(axis, by):
        count = lax.axis_size(axis)
        return [(i, (i + by) % count) for i in range(count)]

    from_left = lax.ppermute(right_side, "col", ring("col", 1))
    from_right = lax.ppermute(left_side, "col", ring("col", -1))
    down_send = jnp.concatenate([down_line, from_left[:, rows - LANES :], from_right[:, rows - LANES :]], axis=1)
    up_send = jnp.concatenate([up_line, from_left[:, :LANES], from_right[:, :LANES]], axis=1)
    from_above = lax.ppermute(down_send, "row", ring("row", 1))
    from_below = lax.ppermute(up_send, "row", ring("row", -1))
    return from_left, from_right, from_above, from_below


def relax_kernel(take, outs, give, flow_ref, initial_ref, trans_ref, share_ref, next_ref, *weight_refs):
    (out_ref,) = outs
    rows, cols = out_ref.shape
    count = cols // LANES
    top, height = PAD, rows + 2 * EDGE
    one, flags = take(0)[0], take(1)
    ok_above, ok_below, ok_left, ok_right = [flags[i] for i in range(4)]
    from_left, from_right, from_above, from_below = [take(6 + i) for i in range(4)]
    fields = (flow_ref, initial_ref, trans_ref, share_ref)
    lane = iota((LANES, LANES), 1)

    def beside(left, right):
        many = len(fields) * EDGE
        fill = jnp.zeros((LANES - 2 * many, LANES), F32)
        block = jnp.transpose(jnp.concatenate([left, right, fill], axis=0))
        out = []
        for at in range(len(fields)):
            on_left = pltpu.roll(block, (LANES - EDGE - at * EDGE) % LANES, 1) * ok_left
            on_right = pltpu.roll(block, (-many - at * EDGE) % LANES, 1) * ok_right
            out.append(jnp.where(lane < EDGE, on_right, jnp.where(lane >= LANES - EDGE, on_left, 0.0)))
        return out

    first_row, last_row = top + EDGE, top + EDGE + rows
    for first in range(0, rows, LANES):
        blocks = beside(from_left[:, first : first + LANES], from_right[:, first : first + LANES])
        for ref, block in zip(fields, blocks):
            ref[count, first_row + first : first_row + first + LANES, :] = block
    above = beside(from_above[:, cols : cols + LANES], from_above[:, cols + LANES :])
    below = beside(from_below[:, cols : cols + LANES], from_below[:, cols + LANES :])
    empty = jnp.zeros((PAD, LANES), F32)
    for at, ref in enumerate(fields):
        part = slice(at * EDGE, (at + 1) * EDGE)
        ref[count, top:first_row, :] = above[at][LANES - EDGE :, :] * ok_above
        ref[count, last_row : last_row + EDGE, :] = below[at][:EDGE, :] * ok_below
        for b in range(count):
            ref[b, top:first_row, :] = from_above[part, b * LANES : (b + 1) * LANES] * ok_above
            ref[b, last_row : last_row + EDGE, :] = from_below[part, b * LANES : (b + 1) * LANES] * ok_below
        for b in range(count + 1):
            ref[b, :top, :] = empty
            ref[b, last_row + EDGE :, :] = empty
    for b in range(count + 1):
        next_ref[b, :top, :] = empty
        next_ref[b, last_row + EDGE :, :] = empty
    for ref, tile in ((flow_ref, take(5)), (trans_ref, take(2)), (share_ref, take(3)), (initial_ref, take(4))):
        for b in range(count):
            ref[b, first_row:last_row, :] = tile[:, b * LANES : (b + 1) * LANES].astype(F32)

    edge = iota((height, LANES), 1)

    def around(ref):
        mid = [ref[b, top : top + height, :] for b in range(count + 1)]
        later = [pltpu.roll(x, 1, 1) for x in mid]
        sooner = [pltpu.roll(x, LANES - 1, 1) for x in mid]
        for b in range(count + 1):
            yield (
                mid[b],
                ref[b, pl.ds(top - one, height), :],
                ref[b, pl.ds(top + one, height), :],
                jnp.where(edge == 0, later[b - 1], later[b]),
                jnp.where(edge == LANES - 1, sooner[(b + 1) % (count + 1)], sooner[b]),
            )

    up_ref, down_ref, left_ref, right_ref = weight_refs
    line = slice(top, top + height)
    for b, (mid, *others) in enumerate(around(trans_ref)):
        sums = [mid + x for x in others]
        total = 0.5 * (sums[0] + sums[1] + sums[2] + sums[3])
        scale = share_ref[b, line, :] / (store_rate + total)
        half = 0.5 * scale
        for ref, x in zip(weight_refs, sums):
            ref[b] = half * x
        flow_ref[b, line, :] = scale * (store_rate * initial_ref[b, line, :] + flow_ref[b, line, :])
    now, later_ref = initial_ref, next_ref
    for sweep in range(SWEEPS):
        for b, (_, above, below, on_left, on_right) in enumerate(around(now)):
            if sweep == SWEEPS - 1 and b == count:
                continue
            inflow = up_ref[b] * above + down_ref[b] * below
            inflow = inflow + left_ref[b] * on_left + right_ref[b] * on_right
            surface = flow_ref[b, line, :] + inflow
            if sweep == SWEEPS - 1:
                out_ref[:, b * LANES : (b + 1) * LANES] = surface[EDGE : EDGE + rows, :]
                give(0, b)
            else:
                later_ref[b, line, :] = surface
        now, later_ref = later_ref, now


def relax(flags, transmit, land_share, initial, flow, sides):
    rows, cols = flow.shape
    many = cols // LANES + 1
    field = pltpu.VMEM((many, rows + 2 * (EDGE + PAD), LANES), F32)
    weight = pltpu.VMEM((many, rows + 2 * EDGE, LANES), F32)
    one = jnp.where(flags[:1] < 2.0, 1, 0).astype(jnp.int32)
    return staged(
        relax_kernel,
        "lateral_relax",
        (one, flags, transmit, land_share, initial, flow) + tuple(sides),
        (floats(rows, cols),),
        [field] * 5 + [weight] * 4,
        6,
        held=range(2, 10),
        in_smem=(0, 1),
        pieces=(cols // LANES,),
        by_lanes=True,
    )[0]


def on_device(precip, head, trans_coef, land, dest, moisture, ksat):
    rows, cols = precip.shape
    row_count = lax.axis_size("row")
    col_count = lax.axis_size("col")
    peers = row_count * col_count
    owned, layers, _ = moisture.shape
    cap = 2 * (rows * cols // LANES) // peers
    axes = ("row", "col")
    moist2 = moisture.reshape(owned * layers, LANES)

    sent, place = pack(dest, precip, head, land, peers, cap, owned)
    wide = (2 * cap + 1) * LANES
    got = lax.all_to_all(sent.reshape(peers, 1, wide), axes, split_axis=0, concat_axis=0, tiled=True)
    got = got.reshape(peers * (2 * cap + 1), LANES)

    initial, left, right, up, down, transmit, land_share = derive(head, trans_coef, land)
    responses = response(moist2, ksat, layers)
    row_at, col_at = lax.axis_index("row"), lax.axis_index("col")
    flags = jnp.stack([row_at > 0, row_at < row_count - 1, col_at > 0, col_at < col_count - 1]).astype(F32)

    infil, share, answer = owner_side(got, responses, peers, cap, (up,))
    back = lax.all_to_all(answer.reshape(peers, cap, LANES), axes, split_axis=0, concat_axis=0, tiled=True)
    back = back.reshape(peers * cap, LANES)
    saturation = saturate(moist2, ksat, infil, share, layers)

    flow, *edges = source_of(back, place, (left, right, up, down), peers, cap, (saturation,))
    left, right, up, down = edges
    surface = relax(flags, transmit, land_share, initial, flow, exchange(up, down, left, right))
    return (saturation.reshape(owned, layers, LANES), surface)


def solution(mesh):
    tile = P("row", "col")
    return jax.shard_map(
        on_device,
        mesh=mesh,
        in_specs=(tile,) * 5 + (P(("row", "col"), None, None), P(("row", "col"), None)),
        out_specs=(P(("row", "col"), None, None), tile),
        check_vma=False,
    )
```

```python
import math

import jax
import jax.numpy as jnp
from jax import lax
from jax.experimental import pallas as pl
from jax.experimental.pallas import tpu as pltpu
from jax.sharding import PartitionSpec as P

SWEEPS = 4
LANES = 128
EDGE = 8
WIDE = 4
PAD = 8
GROUPS = 4

layer_depth = 0.1
step_ratio = 0.1
residual_water = 0.05
pore_range = 0.4
couple_rate = 0.05
recharge_gain = 20.0
store_rate = 0.2

F32 = jnp.float32
BF16 = jnp.bfloat16
MIB = 1 << 20


def iota(shape, dim):
    return lax.broadcasted_iota(jnp.int32, shape, dim)


def params():
    return pltpu.CompilerParams(vmem_limit_bytes=24 * MIB)


def cost(us):
    return pl.CostEstimate(flops=0, bytes_accessed=int(us * 3.0e6), transcendentals=0)


def halves(x):
    high = x.astype(BF16)
    low = (x - high.astype(F32)).astype(BF16)
    return high, low


def hbm(x):
    return pltpu.with_memory_space_constraint(x, pltpu.HBM)


def vmem(x):
    return pltpu.with_memory_space_constraint(x, pltpu.VMEM)


def staged(body, name, ins, outs, scratch, us, after=(), held=(), left=(), pieces=None, by_lanes=False, in_smem=(), small=False):
    n, m, k = len(ins), len(outs), len(after)
    pieces = pieces or (1,) * m
    moved = [i for i in range(n) if i not in held and i not in in_smem]
    sent = [i for i in range(m) if i not in left]

    def kernel(*refs):
        in_at, out_at = refs[:n], refs[n + k : n + k + m]
        rest = refs[n + k + m :]
        in_ref = dict(zip(moved, rest))
        rest = rest[len(moved) :]
        out_ref = dict(enumerate(out_at)) | dict(zip(sent, rest))
        rest = rest[len(sent) :]
        in_sem, out_sem = rest[:2]
        reads = {i: pltpu.make_async_copy(in_at[i], in_ref[i], in_sem.at[i]) for i in moved}
        writes = {}
        for i in sent:
            size = outs[i].shape[by_lanes] // pieces[i]
            for p in range(pieces[i]):
                part = pl.ds(p * size, size)
                part = (slice(None), part) if by_lanes else part
                sem = out_sem.at[sum(pieces[:i]) + p]
                writes[i, p] = pltpu.make_async_copy(out_ref[i].at[part], out_at[i].at[part], sem)
        for read in reads.values():
            read.start()

        def take(i):
            if i not in moved:
                return in_at[i]
            reads[i].wait()
            return in_ref[i]

        body(take, [out_ref[i] for i in range(m)], lambda i, p=0: writes[i, p].start(), *rest[2:])
        for write in writes.values():
            write.wait()

    spaces = {**{i: pltpu.VMEM for i in held}, **{i: pltpu.SMEM for i in in_smem}}
    in_specs = [pl.BlockSpec(memory_space=spaces.get(i, pltpu.HBM)) for i in range(n)]
    placed = [x if i in in_smem else vmem(x) if i in held else hbm(x) for i, x in enumerate(ins)]
    return pl.pallas_call(
        kernel,
        out_shape=tuple(
            pltpu.VMEM(x.shape, x.dtype) if i in left else pltpu.HBM(x.shape, x.dtype) for i, x in enumerate(outs)
        ),
        in_specs=in_specs + [pl.BlockSpec(memory_space=pltpu.VMEM if small else pltpu.HBM)] * k,
        out_specs=tuple(pl.BlockSpec(memory_space=pltpu.VMEM if i in left else pltpu.HBM) for i in range(m)),
        scratch_shapes=[pltpu.VMEM(ins[i].shape, ins[i].dtype) for i in moved]
        + [pltpu.VMEM(outs[i].shape, outs[i].dtype) for i in sent]
        + [pltpu.SemaphoreType.DMA((n,)), pltpu.SemaphoreType.DMA((sum(pieces),))]
        + list(scratch),
        compiler_params=pltpu.CompilerParams(vmem_limit_bytes=40 * MIB),
        cost_estimate=cost(us),
        name=name,
    )(*placed, *[vmem(x) if small else hbm(x) for x in after])


def floats(*shape):
    return jax.ShapeDtypeStruct(shape, F32)


def pack_kernel(peers, cap, owned, rows, cols, take, outs, give, hot_ref, data_ref):
    out_ref, place_ref = outs
    parts = cols // LANES
    blocks = rows * parts
    stride = 2 * cap + 1
    dest_ref = take(0)
    dest = jnp.concatenate([dest_ref[k : k + 1, :] for k in range(parts)], axis=1)
    shift = owned.bit_length() - 1
    owner = dest >> shift
    label = (dest & (owned - 1)) + 1
    owner_hot = owner == iota((peers, blocks), 0)
    before = (iota((LANES, LANES), 0) < iota((LANES, LANES), 1)).astype(F32).astype(BF16)
    carry = jnp.zeros((peers, 1), F32)
    ranks = []
    for chunk in range(blocks // LANES):
        hot = owner_hot[:, chunk * LANES : (chunk + 1) * LANES]
        hot_f = hot.astype(F32)
        count = jnp.dot(hot_f.astype(BF16), before, preferred_element_type=F32) + carry
        ranks.append(jnp.sum(count * hot_f, axis=0, keepdims=True))
        carry = carry + jnp.sum(hot_f, axis=1, keepdims=True)
    rank = jnp.concatenate(ranks, axis=1).astype(jnp.int32)
    place = owner + peers * rank
    place_ref[...] = place
    owner_f = owner_hot.astype(F32)
    rank_hot = (rank == iota((LANES, blocks), 0)).astype(F32).astype(BF16)
    contract = (((1,), (1,)), ((), ()))
    tops = (owner_f * (label >> 5).astype(F32)).astype(BF16)
    lows = (owner_f * (label & 31).astype(F32)).astype(BF16)
    labels = 32.0 * lax.dot_general(tops, rank_hot, contract, preferred_element_type=F32)
    labels = labels + lax.dot_general(lows, rank_hot, contract, preferred_element_type=F32)
    out_ref[pl.ds(2 * cap, peers, stride=stride), :] = labels
    size = peers // GROUPS

    def mark(group):
        for k in range(cap):
            at = (group * cap + k) * size
            hot_ref[at : at + size, :] = (
                (place == iota((size, blocks), 0) + (k * peers + group * size)).astype(F32).astype(BF16)
            )

    mark(0)
    precip_ref, head_ref, land_ref = take(1), take(2), take(3)
    for part in range(parts):
        lane = slice(part * LANES, (part + 1) * LANES)
        line = slice(part * rows, (part + 1) * rows)
        infil = precip_ref[:, lane] * land_ref[:, lane].astype(F32)
        for at, piece in enumerate(halves(infil) + halves(head_ref[:, lane])):
            data_ref[line, at * LANES : (at + 1) * LANES] = piece
    for group in range(GROUPS):
        if group + 1 < GROUPS:
            mark(group + 1)
        line = slice(group * cap * size, (group + 1) * cap * size)
        moved = jnp.dot(hot_ref[line, :], data_ref[...], preferred_element_type=F32)
        for k in range(cap):
            part = moved[k * size : (k + 1) * size]
            row = group * size * stride + k
            out_ref[pl.ds(row, size, stride=stride), :] = part[:, :LANES] + part[:, LANES : 2 * LANES]
            out_ref[pl.ds(row + cap, size, stride=stride), :] = part[:, 2 * LANES : 3 * LANES] + part[:, 3 * LANES :]
        give(0, group)


def pack(dest, precip, head, land, peers, cap, owned):
    rows, cols = precip.shape
    blocks = rows * cols // LANES

    def body(*refs):
        pack_kernel(peers, cap, owned, rows, cols, *refs)

    return staged(
        body,
        "pack_forcing",
        (jnp.transpose(dest), precip, head, land),
        (floats(peers * (2 * cap + 1), LANES), jax.ShapeDtypeStruct((1, blocks), jnp.int32)),
        [pltpu.VMEM((peers * cap, blocks), BF16), pltpu.VMEM((blocks, 4 * LANES), BF16)],
        5,
        pieces=(GROUPS, 1),
        left=(1,),
    )


def layer_terms(moist, half_k, depth_factor):
    wet = moist * (1.0 / pore_range) - residual_water / pore_range
    wet2 = wet * wet
    a = half_k * depth_factor
    t = a * wet2
    return wet, 7.5 * t, t * wet, a + 5.0 * t


def inverse(x):
    return 1.0 / x


def eliminate(layers, load, ksat, infil, response, keep):
    half_k = 0.5 * ksat
    moist = load(0)
    wet, hs, hc, d5 = layer_terms(moist, half_k, math.exp(-0.5 * layer_depth))
    flux_above = infil
    ratio = reduced = resp = hs_prev = g_prev = None
    for k in range(layers):
        last = k == layers - 1
        if not last:
            moist_n = load(k + 1)
            wet_n, hs_n, hc_n, d5_n = layer_terms(
                moist_n, half_k, math.exp(-(k + 1.5) * layer_depth)
            )
            g = d5 + d5_n
            flux = (hc + hc_n) - g * (moist_n - moist)
        if k == 0:
            diagonal = (g + step_ratio) + hs
        elif last:
            diagonal = (g_prev + (step_ratio + couple_rate)) + hs
        else:
            diagonal = (g_prev + step_ratio) + g
        if last:
            bottom = 2.0 * hc + couple_rate * (moist - residual_water)
            right = flux_above - bottom
        else:
            right = (0.0 - flux) if flux_above is None else (flux_above - flux)
        if k == 0:
            inv = inverse(diagonal)
            reduced = right * inv
            resp = inv
        else:
            neg_sub = hs_prev + g_prev
            inv = inverse(diagonal + neg_sub * ratio)
            reduced = (right + neg_sub * reduced) * inv
            if response:
                resp = neg_sub * resp * inv
        if last:
            return bottom, 2.0 * hs + couple_rate, reduced, resp, inv, wet
        ratio = (hs_n - g) * inv
        if keep is not None:
            keep(k, wet, ratio, reduced)
        hs_prev, g_prev = hs, g
        flux_above = flux
        moist, wet, hs, hc, d5 = moist_n, wet_n, hs_n, hc_n, d5_n


def response_kernel(layers, chunk, moist_ref, ksat_ref, alpha_ref, beta_ref, gamma_ref):
    def step(j, carry):
        base = j * (chunk * layers)
        line = pl.ds(j * chunk, chunk)
        load = lambda k: moist_ref[pl.ds(base + k, chunk, stride=layers), :]
        bottom, gain, reduced, resp, inv, _ = eliminate(layers, load, ksat_ref[line, :], None, True, None)
        alpha_ref[line, :] = bottom + gain * reduced
        beta_ref[line, :] = gain * resp
        gamma_ref[line, :] = (couple_rate * pore_range) * (gain * inv - 1.0)
        return carry

    lax.fori_loop(0, ksat_ref.shape[0] // chunk, step, 0)


def response(moist2, ksat, layers):
    owned = ksat.shape[0]
    size = 128

    def kernel(*refs):
        response_kernel(layers, 128, *refs)

    small = pl.BlockSpec((size, LANES), lambda i: (i, 0))
    return pl.pallas_call(
        kernel,
        grid=(owned // size,),
        out_shape=(pltpu.HBM((owned, LANES), F32),) * 3,
        in_specs=[pl.BlockSpec((size * layers, LANES), lambda i: (i, 0)), small],
        out_specs=(small,) * 3,
        compiler_params=params(),
        cost_estimate=cost(13),
        name="column_response",
    )(hbm(moist2), hbm(ksat))


def saturation_kernel(layers, chunk, moist_ref, ksat_ref, infil_ref, share_ref, out_ref, wet_s, ratio_s, reduced_s):
    def step(j, carry):
        base = j * (chunk * layers)
        line = pl.ds(j * chunk, chunk)
        load = lambda k: moist_ref[pl.ds(base + k, chunk, stride=layers), :]

        def keep(k, wet, ratio, reduced):
            wet_s[k] = wet
            ratio_s[k] = ratio
            reduced_s[k] = reduced

        _, _, reduced, _, inv, wet = eliminate(layers, load, ksat_ref[line, :], infil_ref[line, :], False, keep)
        change = reduced + (couple_rate * pore_range) * share_ref[line, :] * inv
        out_ref[pl.ds(base + layers - 1, chunk, stride=layers), :] = wet + (1.0 / pore_range) * change
        for k in range(layers - 2, -1, -1):
            change = reduced_s[k] - ratio_s[k] * change
            out_ref[pl.ds(base + k, chunk, stride=layers), :] = wet_s[k] + (1.0 / pore_range) * change
        return carry

    lax.fori_loop(0, ksat_ref.shape[0] // chunk, step, 0)


def saturate(moist2, ksat, infil, share, layers):
    owned = ksat.shape[0]
    size, chunk = 128, 32

    def kernel(*refs):
        saturation_kernel(layers, chunk, *refs)

    small = pl.BlockSpec((size, LANES), lambda i: (i, 0))
    large = pl.BlockSpec((size * layers, LANES), lambda i: (i, 0))
    return pl.pallas_call(
        kernel,
        grid=(owned // size,),
        out_shape=pltpu.HBM((owned * layers, LANES), F32),
        in_specs=[large, small, small, small],
        out_specs=large,
        scratch_shapes=[pltpu.VMEM((layers - 1, chunk, LANES), F32)] * 3,
        compiler_params=params(),
        cost_estimate=cost(14),
        name="column_saturation",
    )(*[hbm(x) for x in (moist2, ksat, infil, share)])


def owner_kernel(peers, cap, owned, take, outs, give, data_ref, hot_ref, back_ref, rech_ref):
    infil_ref, share_ref, ans_ref = outs
    got_ref = take(0)
    stride = 2 * cap + 1
    labels = got_ref[pl.ds(2 * cap, peers, stride=stride), :]
    turned = jnp.transpose(labels).astype(jnp.int32) - 1
    labels = labels.astype(jnp.int32) - 1
    group = owned // 2

    def mark(first):
        for k in range(cap):
            hot_ref[first : first + group, k * peers : (k + 1) * peers] = (
                (turned[k : k + 1, :] == iota((group, peers), 0) + first).astype(F32).astype(BF16)
            )

    for k in range(cap):
        line = slice(k * peers, (k + 1) * peers)
        pieces = halves(got_ref[pl.ds(k, peers, stride=stride), :])
        pieces = pieces + halves(got_ref[pl.ds(cap + k, peers, stride=stride), :])
        for at, piece in enumerate(pieces):
            data_ref[line, at * LANES : (at + 1) * LANES] = piece
    mark(0)
    alpha_ref, beta_ref, gamma_ref = [take(1 + k) for k in range(3)]
    mark(group)
    for first in range(0, owned, group):
        line = slice(first, first + group)
        moved = jnp.dot(hot_ref[line, :], data_ref[...], preferred_element_type=F32)
        infil = moved[:, :LANES] + moved[:, LANES : 2 * LANES]
        head = moved[:, 2 * LANES : 3 * LANES] + moved[:, 3 * LANES :]
        share = jax.nn.sigmoid(head)
        infil_ref[line, :] = infil
        share_ref[line, :] = share
        rech = alpha_ref[line, :] + beta_ref[line, :] * infil + gamma_ref[line, :] * share
        high, low = halves(rech)
        rech_ref[line, :LANES] = high
        rech_ref[line, LANES:] = low
    size = peers // GROUPS
    for turn in range(GROUPS):
        first = turn * size
        for k in range(cap):
            at = first * cap + k * size
            back_ref[at : at + size, :] = (
                (labels[first : first + size, k : k + 1] == iota((size, owned), 1)).astype(F32).astype(BF16)
            )
    for turn in range(GROUPS):
        first = turn * size
        line = slice(first * cap, (first + size) * cap)
        moved = jnp.dot(back_ref[line, :], rech_ref[...], preferred_element_type=F32)
        for k in range(cap):
            part = moved[k * size : (k + 1) * size]
            ans_ref[pl.ds(first * cap + k, size, stride=cap), :] = part[:, :LANES] + part[:, LANES:]
        if turn == 1:
            give(0)
            give(1)
            give(2, 0)
        if turn > 0:
            give(2, turn)


def owner_side(got, responses, peers, cap, after):
    owned = responses[0].shape[0]

    def body(*refs):
        owner_kernel(peers, cap, owned, *refs)

    return staged(
        body,
        "owner_side",
        (got,) + tuple(responses),
        (floats(owned, LANES), floats(owned, LANES), floats(peers * cap, LANES)),
        [
            pltpu.VMEM((peers * cap, 4 * LANES), BF16),
            pltpu.VMEM((owned, peers * cap), BF16),
            pltpu.VMEM((peers * cap, owned), BF16),
            pltpu.VMEM((owned, 2 * LANES), BF16),
        ],
        8,
        after,
        held=(0,),
        pieces=(1, 1, GROUPS),
        small=True,
    )


def ordered(even, low, high):
    odd = 1.0 - even
    return even * high + odd * low, even * low + odd * high


def sides_of(first, last, even):
    return ordered(even, jnp.transpose(first)[:WIDE, :], jnp.transpose(last)[LANES - WIDE :, :])


def unpack(place_f, data_ref, hot_ref, blocks, peers, cap):
    eye = iota((LANES, LANES), 0) == iota((LANES, LANES), 1)
    for first in range(0, blocks, LANES):
        column = jnp.sum(jnp.where(eye, place_f[:, first : first + LANES], 0.0), axis=1, keepdims=True)
        column = column.astype(jnp.int32)
        for k in range(cap):
            hot_ref[first : first + LANES, k * peers : (k + 1) * peers] = (
                (column == iota((LANES, peers), 1) + k * peers).astype(F32).astype(BF16)
            )
    moved = jnp.dot(hot_ref[:blocks, :], data_ref[...], preferred_element_type=F32)
    return recharge_gain * (moved[:, :LANES] + moved[:, LANES:])


def outer_kernel(peers, cap, rows, cols, take, outs, give, hot_ref):
    first_ref, last_ref, data_ref, *edge_refs = outs
    back_ref = take(0)
    for k in range(cap):
        line = slice(k * peers, (k + 1) * peers)
        high, low = halves(back_ref[pl.ds(k, peers, stride=cap), :])
        data_ref[line, :LANES] = high
        data_ref[line, LANES:] = low
    place_f = take(1)[...].astype(F32)
    flags = take(4)
    last_at = rows * (cols // LANES - 1)
    first = unpack(place_f[:, :rows], data_ref, hot_ref.at[:rows], rows, peers, cap)
    last = unpack(place_f[:, last_at:], data_ref, hot_ref.at[rows:], rows, peers, cap)
    first_ref[...] = first
    last_ref[...] = last
    for ref, raw, x in zip(edge_refs, (take(2), take(3)), sides_of(first, last, flags[4])):
        ref[...] = jnp.concatenate([x, raw[...]], axis=0)


def inner_kernel(peers, cap, take, outs, give, hot_ref):
    flow_ref, *edge_refs = outs
    rows, cols = flow_ref.shape
    first_ref, last_ref, data_ref = take(0), take(1), take(2)
    flags = take(6)
    flow_ref[:, :LANES] = first_ref[...]
    flow_ref[:, cols - LANES :] = last_ref[...]
    place_f = take(3)[...].astype(F32)
    for part in range(1, cols // LANES - 1):
        at = (part - 1) * rows
        flow_ref[:, part * LANES : (part + 1) * LANES] = unpack(
            place_f[:, part * rows : (part + 1) * rows], data_ref, hot_ref.at[at : at + rows], rows, peers, cap
        )
    lines = ordered(flags[5], flow_ref[:WIDE, :], flow_ref[rows - WIDE :, :])
    for ref, raw, x in zip(edge_refs, (take(4), take(5)), lines):
        ref[...] = jnp.concatenate([x, raw[...]], axis=0)


def outer_flow(back, place, sides, flags, cols, peers, cap, after):
    rows = sides[0].shape[1]
    block, side = floats(rows, LANES), floats(4 * WIDE, rows)

    def body(*refs):
        outer_kernel(peers, cap, rows, cols, *refs)

    return staged(
        body,
        "outer_flow",
        (back, place) + tuple(sides) + (flags,),
        (block, block, jax.ShapeDtypeStruct((peers * cap, 2 * LANES), BF16), side, side),
        [pltpu.VMEM((2 * rows, peers * cap), BF16)],
        2,
        after,
        held=(0, 1, 2, 3),
        in_smem=(4,),
        left=range(5),
    )


def inner_flow(first, last, data, place, lines, flags, peers, cap):
    rows, cols = first.shape[0], lines[0].shape[1]
    line = floats(4 * WIDE, cols)

    def body(*refs):
        inner_kernel(peers, cap, *refs)

    return staged(
        body,
        "inner_flow",
        (first, last, data, place) + tuple(lines) + (flags,),
        (floats(rows, cols), line, line),
        [pltpu.VMEM((rows * (cols // LANES - 2), peers * cap), BF16)],
        2,
        held=range(6),
        in_smem=(6,),
        left=range(3),
    )


def derive_kernel(take, outs, give):
    initial_ref, transmit_ref, share_ref, *edge_refs = outs
    rows, cols = initial_ref.shape
    flags = take(3)
    head = take(0)[...]
    share = take(2)[...].astype(F32)
    initial_ref[...] = head * share
    share_ref[...] = share
    transmit_ref[...] = take(1)[...] * (1.0 + 0.5 * jnp.tanh(head))
    for at, x in enumerate((initial_ref, transmit_ref, share_ref)):
        sent = sides_of(x[:, :LANES], x[:, cols - LANES :], flags[4])
        sent = sent + ordered(flags[5], x[:WIDE, :], x[rows - WIDE :, :])
        for ref, y in zip(edge_refs, sent):
            ref[at * WIDE : (at + 1) * WIDE, :] = y


def derive(head, trans_coef, land, flags):
    rows, cols = head.shape
    tile, side, line = floats(rows, cols), floats(3 * WIDE, rows), floats(3 * WIDE, cols)
    return staged(
        derive_kernel,
        "derive_tile",
        (head, trans_coef, land, flags),
        (tile, tile, tile, side, side, line, line),
        [],
        2,
        in_smem=(3,),
        left=range(7),
    )


def partners(axis):
    count = lax.axis_size(axis)
    return [(i, i ^ 1) for i in range(count)], [(i, (i + (1 if i % 2 else -1)) % count) for i in range(count)]


def swap(sides, axis):
    return tuple(lax.ppermute(x, axis, pairs) for x, pairs in zip(sides, partners(axis)))


def with_corners(lines, got):
    rows = got[0].shape[1]
    even = lax.axis_index("row") % 2 == 0
    ends = [(x[:, :LANES], x[:, rows - LANES :]) for x in got]
    to_first = [jnp.where(even, bottom, top) for top, bottom in ends]
    to_second = [jnp.where(even, top, bottom) for top, bottom in ends]
    return jnp.concatenate([lines[0], *to_first], axis=1), jnp.concatenate([lines[1], *to_second], axis=1)


def relax_kernel(take, outs, give, flow_ref, initial_ref, trans_ref, share_ref, next_ref, *weight_refs):
    (out_ref,) = outs
    rows, cols = out_ref.shape
    count = cols // LANES
    top, height = PAD, rows + 2 * EDGE
    one, flags = take(0)[0], take(1)
    ok_above, ok_below, ok_left, ok_right = [flags[i] for i in range(4)]
    from_right, from_left = ordered(flags[4], take(7)[...], take(6)[...])
    from_below, from_above = ordered(flags[5], take(9)[...], take(8)[...])
    fields = (flow_ref, initial_ref, trans_ref, share_ref)
    lane = iota((LANES, LANES), 1)

    def beside(left, right):
        many = len(fields) * WIDE
        fill = jnp.zeros((LANES - 2 * many, LANES), F32)
        block = jnp.transpose(jnp.concatenate([left, right, fill], axis=0))
        out = []
        for at in range(len(fields)):
            on_left = pltpu.roll(block, (LANES - WIDE - at * WIDE) % LANES, 1) * ok_left
            on_right = pltpu.roll(block, (-many - at * WIDE) % LANES, 1) * ok_right
            out.append(jnp.where(lane < WIDE, on_right, jnp.where(lane >= LANES - WIDE, on_left, 0.0)))
        return out

    first_row, last_row = top + EDGE, top + EDGE + rows
    for first in range(0, rows, LANES):
        blocks = beside(from_left[:, first : first + LANES], from_right[:, first : first + LANES])
        for ref, block in zip(fields, blocks):
            ref[count, first_row + first : first_row + first + LANES, :] = block
    corners = []
    for line in (from_above, from_below):
        on_right, on_left = ordered(flags[4], line[:, cols + LANES :], line[:, cols : cols + LANES])
        corners.append(beside(on_left, on_right))
    above, below = corners
    empty = jnp.zeros((PAD + EDGE, LANES), F32)
    for at, ref in enumerate(fields):
        part = slice(at * WIDE, (at + 1) * WIDE)
        for b in range(count + 1):
            ref[b, :first_row, :] = empty
            ref[b, last_row:, :] = empty
        before, after = slice(first_row - WIDE, first_row), slice(last_row, last_row + WIDE)
        ref[count, before, :] = above[at][LANES - WIDE :, :] * ok_above
        ref[count, after, :] = below[at][:WIDE, :] * ok_below
        for b in range(count):
            ref[b, before, :] = from_above[part, b * LANES : (b + 1) * LANES] * ok_above
            ref[b, after, :] = from_below[part, b * LANES : (b + 1) * LANES] * ok_below
    for b in range(count + 1):
        next_ref[b, :first_row, :] = empty
        next_ref[b, last_row:, :] = empty
    for ref, tile in ((flow_ref, take(5)), (trans_ref, take(2)), (share_ref, take(3)), (initial_ref, take(4))):
        for b in range(count):
            ref[b, first_row:last_row, :] = tile[:, b * LANES : (b + 1) * LANES].astype(F32)

    edge = iota((height, LANES), 1)

    def around(ref):
        mid = [ref[b, top : top + height, :] for b in range(count + 1)]
        later = [pltpu.roll(x, 1, 1) for x in mid]
        sooner = [pltpu.roll(x, LANES - 1, 1) for x in mid]
        for b in range(count + 1):
            yield (
                mid[b],
                ref[b, pl.ds(top - one, height), :],
                ref[b, pl.ds(top + one, height), :],
                jnp.where(edge == 0, later[b - 1], later[b]),
                jnp.where(edge == LANES - 1, sooner[(b + 1) % (count + 1)], sooner[b]),
            )

    up_ref, down_ref, left_ref, right_ref = weight_refs
    line = slice(top, top + height)
    for b, (mid, *others) in enumerate(around(trans_ref)):
        sums = [mid + x for x in others]
        total = 0.5 * (sums[0] + sums[1] + sums[2] + sums[3])
        scale = share_ref[b, line, :] / (store_rate + total)
        half = 0.5 * scale
        for ref, x in zip(weight_refs, sums):
            ref[b] = half * x
        flow_ref[b, line, :] = scale * (store_rate * initial_ref[b, line, :] + flow_ref[b, line, :])
    now, later_ref = initial_ref, next_ref
    for sweep in range(SWEEPS):
        for b, (_, above, below, on_left, on_right) in enumerate(around(now)):
            if sweep == SWEEPS - 1 and b == count:
                continue
            inflow = up_ref[b] * above + down_ref[b] * below
            inflow = inflow + left_ref[b] * on_left + right_ref[b] * on_right
            surface = flow_ref[b, line, :] + inflow
            if sweep == SWEEPS - 1:
                out_ref[:, b * LANES : (b + 1) * LANES] = surface[EDGE : EDGE + rows, :]
                give(0, b)
            else:
                later_ref[b, line, :] = surface
        now, later_ref = later_ref, now


def relax(flags, transmit, land_share, initial, flow, sides):
    rows, cols = flow.shape
    many = cols // LANES + 1
    field = pltpu.VMEM((many, rows + 2 * (EDGE + PAD), LANES), F32)
    weight = pltpu.VMEM((many, rows + 2 * EDGE, LANES), F32)
    one = jnp.where(flags[:1] < 2.0, 1, 0).astype(jnp.int32)
    return staged(
        relax_kernel,
        "lateral_relax",
        (one, flags, transmit, land_share, initial, flow) + tuple(sides),
        (floats(rows, cols),),
        [field] * 5 + [weight] * 4,
        6,
        held=range(2, 10),
        in_smem=(0, 1),
        pieces=(cols // LANES,),
        by_lanes=True,
    )[0]


def on_device(precip, head, trans_coef, land, dest, moisture, ksat):
    rows, cols = precip.shape
    row_count = lax.axis_size("row")
    col_count = lax.axis_size("col")
    peers = row_count * col_count
    owned, layers, _ = moisture.shape
    cap = 2 * (rows * cols // LANES) // peers
    axes = ("row", "col")
    moist2 = moisture.reshape(owned * layers, LANES)

    sent, place = pack(dest, precip, head, land, peers, cap, owned)
    wide = (2 * cap + 1) * LANES
    got = lax.all_to_all(sent.reshape(peers, 1, wide), axes, split_axis=0, concat_axis=0, tiled=True)
    got = got.reshape(peers * (2 * cap + 1), LANES)

    row_at, col_at = lax.axis_index("row"), lax.axis_index("col")
    flags = [row_at > 0, row_at < row_count - 1, col_at > 0, col_at < col_count - 1, col_at % 2 == 0, row_at % 2 == 0]
    flags = jnp.stack(flags).astype(F32)
    initial, transmit, land_share, *edges = derive(head, trans_coef, land, flags)
    responses = response(moist2, ksat, layers)

    infil, share, answer = owner_side(got, responses, peers, cap, (edges[0],))
    back = lax.all_to_all(answer.reshape(peers, cap, LANES), axes, split_axis=0, concat_axis=0, tiled=True)
    back = back.reshape(peers * cap, LANES)
    saturation = saturate(moist2, ksat, infil, share, layers)

    first, last, data, *sides = outer_flow(back, place, edges[:2], flags, cols, peers, cap, (saturation,))
    got_sides = swap(sides, "col")
    flow, *lines = inner_flow(first, last, data, place, edges[2:], flags, peers, cap)
    got_lines = swap(with_corners(lines, got_sides), "row")
    surface = relax(flags, transmit, land_share, initial, flow, got_sides + got_lines)
    return (saturation.reshape(owned, layers, LANES), surface)


def solution(mesh):
    tile = P("row", "col")
    return jax.shard_map(
        on_device,
        mesh=mesh,
        in_specs=(tile,) * 5 + (P(("row", "col"), None, None), P(("row", "col"), None)),
        out_specs=(P(("row", "col"), None, None), tile),
        check_vma=False,
    )
```

```python
import math

import jax
import jax.numpy as jnp
from jax import lax
from jax.experimental import pallas as pl
from jax.experimental.pallas import tpu as pltpu
from jax.sharding import PartitionSpec as P

SWEEPS = 4
LANES = 128
EDGE = 8
WIDE = 4
PAD = 8
GROUPS = 4

layer_depth = 0.1
step_ratio = 0.1
residual_water = 0.05
pore_range = 0.4
couple_rate = 0.05
recharge_gain = 20.0
store_rate = 0.2

F32 = jnp.float32
BF16 = jnp.bfloat16
MIB = 1 << 20


def iota(shape, dim):
    return lax.broadcasted_iota(jnp.int32, shape, dim)


def params():
    return pltpu.CompilerParams(vmem_limit_bytes=24 * MIB)


def cost(us):
    return pl.CostEstimate(flops=0, bytes_accessed=int(us * 3.0e6), transcendentals=0)


def halves(x):
    high = x.astype(BF16)
    low = (x - high.astype(F32)).astype(BF16)
    return high, low


def hbm(x):
    return pltpu.with_memory_space_constraint(x, pltpu.HBM)


def vmem(x):
    return pltpu.with_memory_space_constraint(x, pltpu.VMEM)


def staged(body, name, ins, outs, scratch, us, after=(), held=(), left=(), pieces=None, by_lanes=False, in_smem=(), small=False):
    n, m, k = len(ins), len(outs), len(after)
    pieces = pieces or (1,) * m
    moved = [i for i in range(n) if i not in held and i not in in_smem]
    sent = [i for i in range(m) if i not in left]

    def kernel(*refs):
        in_at, out_at = refs[:n], refs[n + k : n + k + m]
        rest = refs[n + k + m :]
        in_ref = dict(zip(moved, rest))
        rest = rest[len(moved) :]
        out_ref = dict(enumerate(out_at)) | dict(zip(sent, rest))
        rest = rest[len(sent) :]
        in_sem, out_sem = rest[:2]
        reads = {i: pltpu.make_async_copy(in_at[i], in_ref[i], in_sem.at[i]) for i in moved}
        writes = {}
        for i in sent:
            size = outs[i].shape[by_lanes] // pieces[i]
            for p in range(pieces[i]):
                part = pl.ds(p * size, size)
                part = (slice(None), part) if by_lanes else part
                sem = out_sem.at[sum(pieces[:i]) + p]
                writes[i, p] = pltpu.make_async_copy(out_ref[i].at[part], out_at[i].at[part], sem)
        for read in reads.values():
            read.start()

        def take(i):
            if i not in moved:
                return in_at[i]
            reads[i].wait()
            return in_ref[i]

        body(take, [out_ref[i] for i in range(m)], lambda i, p=0: writes[i, p].start(), *rest[2:])
        for write in writes.values():
            write.wait()

    spaces = {**{i: pltpu.VMEM for i in held}, **{i: pltpu.SMEM for i in in_smem}}
    in_specs = [pl.BlockSpec(memory_space=spaces.get(i, pltpu.HBM)) for i in range(n)]
    placed = [x if i in in_smem else vmem(x) if i in held else hbm(x) for i, x in enumerate(ins)]
    return pl.pallas_call(
        kernel,
        out_shape=tuple(
            pltpu.VMEM(x.shape, x.dtype) if i in left else pltpu.HBM(x.shape, x.dtype) for i, x in enumerate(outs)
        ),
        in_specs=in_specs + [pl.BlockSpec(memory_space=pltpu.VMEM if small else pltpu.HBM)] * k,
        out_specs=tuple(pl.BlockSpec(memory_space=pltpu.VMEM if i in left else pltpu.HBM) for i in range(m)),
        scratch_shapes=[pltpu.VMEM(ins[i].shape, ins[i].dtype) for i in moved]
        + [pltpu.VMEM(outs[i].shape, outs[i].dtype) for i in sent]
        + [pltpu.SemaphoreType.DMA((n,)), pltpu.SemaphoreType.DMA((sum(pieces),))]
        + list(scratch),
        compiler_params=pltpu.CompilerParams(vmem_limit_bytes=40 * MIB),
        cost_estimate=cost(us),
        name=name,
    )(*placed, *[vmem(x) if small else hbm(x) for x in after])


def floats(*shape):
    return jax.ShapeDtypeStruct(shape, F32)


def pack_kernel(peers, cap, owned, rows, cols, take, outs, give, hot_ref, data_ref):
    out_ref, place_ref = outs
    parts = cols // LANES
    blocks = rows * parts
    stride = 2 * cap + 1
    dest_ref = take(0)
    dest = jnp.concatenate([dest_ref[k : k + 1, :] for k in range(parts)], axis=1)
    shift = owned.bit_length() - 1
    owner = dest >> shift
    label = (dest & (owned - 1)) + 1
    owner_hot = owner == iota((peers, blocks), 0)
    before = (iota((LANES, LANES), 0) < iota((LANES, LANES), 1)).astype(F32).astype(BF16)
    carry = jnp.zeros((peers, 1), F32)
    ranks = []
    for chunk in range(blocks // LANES):
        hot = owner_hot[:, chunk * LANES : (chunk + 1) * LANES]
        hot_f = hot.astype(F32)
        count = jnp.dot(hot_f.astype(BF16), before, preferred_element_type=F32) + carry
        ranks.append(jnp.sum(count * hot_f, axis=0, keepdims=True))
        carry = carry + jnp.sum(hot_f, axis=1, keepdims=True)
    rank = jnp.concatenate(ranks, axis=1).astype(jnp.int32)
    place = owner + peers * rank
    place_ref[...] = place
    owner_f = owner_hot.astype(F32)
    rank_hot = (rank == iota((LANES, blocks), 0)).astype(F32).astype(BF16)
    contract = (((1,), (1,)), ((), ()))
    tops = (owner_f * (label >> 5).astype(F32)).astype(BF16)
    lows = (owner_f * (label & 31).astype(F32)).astype(BF16)
    labels = 32.0 * lax.dot_general(tops, rank_hot, contract, preferred_element_type=F32)
    labels = labels + lax.dot_general(lows, rank_hot, contract, preferred_element_type=F32)
    out_ref[pl.ds(2 * cap, peers, stride=stride), :] = labels
    size = peers // GROUPS

    def mark(group):
        for k in range(cap):
            at = (group * cap + k) * size
            hot_ref[at : at + size, :] = (
                (place == iota((size, blocks), 0) + (k * peers + group * size)).astype(F32).astype(BF16)
            )

    mark(0)
    precip_ref, head_ref, land_ref = take(1), take(2), take(3)
    for part in range(parts):
        lane = slice(part * LANES, (part + 1) * LANES)
        line = slice(part * rows, (part + 1) * rows)
        infil = precip_ref[:, lane] * land_ref[:, lane].astype(F32)
        for at, piece in enumerate(halves(infil) + halves(head_ref[:, lane])):
            data_ref[line, at * LANES : (at + 1) * LANES] = piece
    for group in range(GROUPS):
        if group + 1 < GROUPS:
            mark(group + 1)
        line = slice(group * cap * size, (group + 1) * cap * size)
        moved = jnp.dot(hot_ref[line, :], data_ref[...], preferred_element_type=F32)
        for k in range(cap):
            part = moved[k * size : (k + 1) * size]
            row = group * size * stride + k
            out_ref[pl.ds(row, size, stride=stride), :] = part[:, :LANES] + part[:, LANES : 2 * LANES]
            out_ref[pl.ds(row + cap, size, stride=stride), :] = part[:, 2 * LANES : 3 * LANES] + part[:, 3 * LANES :]
        give(0, group)


def pack(dest, precip, head, land, peers, cap, owned):
    rows, cols = precip.shape
    blocks = rows * cols // LANES

    def body(*refs):
        pack_kernel(peers, cap, owned, rows, cols, *refs)

    return staged(
        body,
        "pack_forcing",
        (jnp.transpose(dest), precip, head, land),
        (floats(peers * (2 * cap + 1), LANES), jax.ShapeDtypeStruct((1, blocks), jnp.int32)),
        [pltpu.VMEM((peers * cap, blocks), BF16), pltpu.VMEM((blocks, 4 * LANES), BF16)],
        5,
        pieces=(GROUPS, 1),
        left=(1,),
    )


def layer_terms(moist, half_k, depth_factor):
    wet = moist * (1.0 / pore_range) - residual_water / pore_range
    wet2 = wet * wet
    a = half_k * depth_factor
    t = a * wet2
    return wet, 7.5 * t, t * wet, a + 5.0 * t


def inverse(x):
    return 1.0 / x


def eliminate(layers, load, ksat, infil, response, keep):
    half_k = 0.5 * ksat
    moist = load(0)
    wet, hs, hc, d5 = layer_terms(moist, half_k, math.exp(-0.5 * layer_depth))
    flux_above = infil
    ratio = reduced = resp = hs_prev = g_prev = None
    for k in range(layers):
        last = k == layers - 1
        if not last:
            moist_n = load(k + 1)
            wet_n, hs_n, hc_n, d5_n = layer_terms(
                moist_n, half_k, math.exp(-(k + 1.5) * layer_depth)
            )
            g = d5 + d5_n
            flux = (hc + hc_n) - g * (moist_n - moist)
        if k == 0:
            diagonal = (g + step_ratio) + hs
        elif last:
            diagonal = (g_prev + (step_ratio + couple_rate)) + hs
        else:
            diagonal = (g_prev + step_ratio) + g
        if last:
            bottom = 2.0 * hc + couple_rate * (moist - residual_water)
            right = flux_above - bottom
        else:
            right = (0.0 - flux) if flux_above is None else (flux_above - flux)
        if k == 0:
            inv = inverse(diagonal)
            reduced = right * inv
            resp = inv
        else:
            neg_sub = hs_prev + g_prev
            inv = inverse(diagonal + neg_sub * ratio)
            reduced = (right + neg_sub * reduced) * inv
            if response:
                resp = neg_sub * resp * inv
        if last:
            return bottom, 2.0 * hs + couple_rate, reduced, resp, inv, wet
        ratio = (hs_n - g) * inv
        if keep is not None:
            keep(k, wet, ratio, reduced)
        hs_prev, g_prev = hs, g
        flux_above = flux
        moist, wet, hs, hc, d5 = moist_n, wet_n, hs_n, hc_n, d5_n


def response_kernel(layers, chunk, moist_ref, ksat_ref, alpha_ref, beta_ref, gamma_ref):
    def step(j, carry):
        base = j * (chunk * layers)
        line = pl.ds(j * chunk, chunk)
        load = lambda k: moist_ref[pl.ds(base + k, chunk, stride=layers), :]
        bottom, gain, reduced, resp, inv, _ = eliminate(layers, load, ksat_ref[line, :], None, True, None)
        alpha_ref[line, :] = bottom + gain * reduced
        beta_ref[line, :] = gain * resp
        gamma_ref[line, :] = (couple_rate * pore_range) * (gain * inv - 1.0)
        return carry

    lax.fori_loop(0, ksat_ref.shape[0] // chunk, step, 0)


def response(moist2, ksat, layers):
    owned = ksat.shape[0]
    size = 128

    def kernel(*refs):
        response_kernel(layers, 128, *refs)

    small = pl.BlockSpec((size, LANES), lambda i: (i, 0))
    return pl.pallas_call(
        kernel,
        grid=(owned // size,),
        out_shape=(pltpu.HBM((owned, LANES), F32),) * 3,
        in_specs=[pl.BlockSpec((size * layers, LANES), lambda i: (i, 0)), small],
        out_specs=(small,) * 3,
        compiler_params=params(),
        cost_estimate=cost(13),
        name="column_response",
    )(hbm(moist2), hbm(ksat))


def saturation_kernel(layers, chunk, moist_ref, ksat_ref, infil_ref, share_ref, out_ref, wet_s, ratio_s, reduced_s):
    def step(j, carry):
        base = j * (chunk * layers)
        line = pl.ds(j * chunk, chunk)
        load = lambda k: moist_ref[pl.ds(base + k, chunk, stride=layers), :]

        def keep(k, wet, ratio, reduced):
            wet_s[k] = wet
            ratio_s[k] = ratio
            reduced_s[k] = reduced

        _, _, reduced, _, inv, wet = eliminate(layers, load, ksat_ref[line, :], infil_ref[line, :], False, keep)
        change = reduced + (couple_rate * pore_range) * share_ref[line, :] * inv
        out_ref[pl.ds(base + layers - 1, chunk, stride=layers), :] = wet + (1.0 / pore_range) * change
        for k in range(layers - 2, -1, -1):
            change = reduced_s[k] - ratio_s[k] * change
            out_ref[pl.ds(base + k, chunk, stride=layers), :] = wet_s[k] + (1.0 / pore_range) * change
        return carry

    lax.fori_loop(0, ksat_ref.shape[0] // chunk, step, 0)


def saturate(moist2, ksat, infil, share, layers):
    owned = ksat.shape[0]
    size, chunk = 128, 32

    def kernel(*refs):
        saturation_kernel(layers, chunk, *refs)

    small = pl.BlockSpec((size, LANES), lambda i: (i, 0))
    large = pl.BlockSpec((size * layers, LANES), lambda i: (i, 0))
    return pl.pallas_call(
        kernel,
        grid=(owned // size,),
        out_shape=pltpu.HBM((owned * layers, LANES), F32),
        in_specs=[large, small, small, small],
        out_specs=large,
        scratch_shapes=[pltpu.VMEM((layers - 1, chunk, LANES), F32)] * 3,
        compiler_params=params(),
        cost_estimate=cost(14),
        name="column_saturation",
    )(*[hbm(x) for x in (moist2, ksat, infil, share)])


def owner_kernel(peers, cap, owned, take, outs, give, data_ref, hot_ref, back_ref, rech_ref):
    infil_ref, share_ref, ans_ref = outs
    got_ref = take(0)
    stride = 2 * cap + 1
    labels = got_ref[pl.ds(2 * cap, peers, stride=stride), :]
    turned = jnp.transpose(labels).astype(jnp.int32) - 1
    labels = labels.astype(jnp.int32) - 1
    group = owned // 2

    def mark(first):
        for k in range(cap):
            hot_ref[first : first + group, k * peers : (k + 1) * peers] = (
                (turned[k : k + 1, :] == iota((group, peers), 0) + first).astype(F32).astype(BF16)
            )

    for k in range(cap):
        line = slice(k * peers, (k + 1) * peers)
        pieces = halves(got_ref[pl.ds(k, peers, stride=stride), :])
        pieces = pieces + halves(got_ref[pl.ds(cap + k, peers, stride=stride), :])
        for at, piece in enumerate(pieces):
            data_ref[line, at * LANES : (at + 1) * LANES] = piece
    size = peers // GROUPS

    def mark_back(first):
        for k in range(cap):
            at = first * cap + k * size
            back_ref[at : at + size, :] = (
                (labels[first : first + size, k : k + 1] == iota((size, owned), 1)).astype(F32).astype(BF16)
            )

    mark(0)
    for first in range(0, owned, group):
        line = slice(first, first + group)
        if first + group < owned:
            mark(first + group)
        moved = jnp.dot(hot_ref[line, :], data_ref[...], preferred_element_type=F32)
        infil_ref[line, :] = moved[:, :LANES] + moved[:, LANES : 2 * LANES]
        share_ref[line, :] = jax.nn.sigmoid(moved[:, 2 * LANES : 3 * LANES] + moved[:, 3 * LANES :])
    alpha_ref, beta_ref, gamma_ref = [take(1 + k) for k in range(3)]
    rech = alpha_ref[...] + beta_ref[...] * infil_ref[...] + gamma_ref[...] * share_ref[...]
    high, low = halves(rech)
    rech_ref[:, :LANES] = high
    rech_ref[:, LANES:] = low
    mark_back(0)
    for turn in range(GROUPS):
        first = turn * size
        if turn + 1 < GROUPS:
            mark_back(first + size)
        line = slice(first * cap, (first + size) * cap)
        moved = jnp.dot(back_ref[line, :], rech_ref[...], preferred_element_type=F32)
        for k in range(cap):
            part = moved[k * size : (k + 1) * size]
            ans_ref[pl.ds(first * cap + k, size, stride=cap), :] = part[:, :LANES] + part[:, LANES:]
        if turn == 1:
            give(2, 0)
            give(2, 1)
            give(0)
            give(1)
        if turn > 1:
            give(2, turn)


def owner_side(got, responses, peers, cap, after):
    owned = responses[0].shape[0]

    def body(*refs):
        owner_kernel(peers, cap, owned, *refs)

    return staged(
        body,
        "owner_side",
        (got,) + tuple(responses),
        (floats(owned, LANES), floats(owned, LANES), floats(peers * cap, LANES)),
        [
            pltpu.VMEM((peers * cap, 4 * LANES), BF16),
            pltpu.VMEM((owned, peers * cap), BF16),
            pltpu.VMEM((peers * cap, owned), BF16),
            pltpu.VMEM((owned, 2 * LANES), BF16),
        ],
        8,
        after,
        held=(0,),
        pieces=(1, 1, GROUPS),
        small=True,
    )


def ordered(even, low, high):
    odd = 1.0 - even
    return even * high + odd * low, even * low + odd * high


def sides_of(first, last, even):
    return ordered(even, jnp.transpose(first)[:WIDE, :], jnp.transpose(last)[LANES - WIDE :, :])


def unpack(place_f, data_ref, hot_ref, blocks, peers, cap):
    eye = iota((LANES, LANES), 0) == iota((LANES, LANES), 1)
    for first in range(0, blocks, LANES):
        column = jnp.sum(jnp.where(eye, place_f[:, first : first + LANES], 0.0), axis=1, keepdims=True)
        column = column.astype(jnp.int32)
        for k in range(cap):
            hot_ref[first : first + LANES, k * peers : (k + 1) * peers] = (
                (column == iota((LANES, peers), 1) + k * peers).astype(F32).astype(BF16)
            )
    moved = jnp.dot(hot_ref[:blocks, :], data_ref[...], preferred_element_type=F32)
    return recharge_gain * (moved[:, :LANES] + moved[:, LANES:])


def outer_kernel(peers, cap, rows, cols, take, outs, give, hot_ref):
    first_ref, last_ref, data_ref, *edge_refs = outs
    back_ref = take(0)
    for k in range(cap):
        line = slice(k * peers, (k + 1) * peers)
        high, low = halves(back_ref[pl.ds(k, peers, stride=cap), :])
        data_ref[line, :LANES] = high
        data_ref[line, LANES:] = low
    place_f = take(1)[...].astype(F32)
    flags = take(4)
    last_at = rows * (cols // LANES - 1)
    first = unpack(place_f[:, :rows], data_ref, hot_ref.at[:rows], rows, peers, cap)
    last = unpack(place_f[:, last_at:], data_ref, hot_ref.at[rows:], rows, peers, cap)
    first_ref[...] = first
    last_ref[...] = last
    for ref, raw, x in zip(edge_refs, (take(2), take(3)), sides_of(first, last, flags[4])):
        ref[...] = jnp.concatenate([x, raw[...]], axis=0)


def inner_kernel(peers, cap, take, outs, give, hot_ref):
    flow_ref, *edge_refs = outs
    rows, cols = flow_ref.shape
    first_ref, last_ref, data_ref = take(0), take(1), take(2)
    flags = take(6)
    flow_ref[:, :LANES] = first_ref[...]
    flow_ref[:, cols - LANES :] = last_ref[...]
    place_f = take(3)[...].astype(F32)
    for part in range(1, cols // LANES - 1):
        at = (part - 1) * rows
        flow_ref[:, part * LANES : (part + 1) * LANES] = unpack(
            place_f[:, part * rows : (part + 1) * rows], data_ref, hot_ref.at[at : at + rows], rows, peers, cap
        )
    lines = ordered(flags[5], flow_ref[:WIDE, :], flow_ref[rows - WIDE :, :])
    for ref, raw, x in zip(edge_refs, (take(4), take(5)), lines):
        ref[...] = jnp.concatenate([x, raw[...]], axis=0)


def outer_flow(back, place, sides, flags, cols, peers, cap, after):
    rows = sides[0].shape[1]
    block, side = floats(rows, LANES), floats(4 * WIDE, rows)

    def body(*refs):
        outer_kernel(peers, cap, rows, cols, *refs)

    return staged(
        body,
        "outer_flow",
        (back, place) + tuple(sides) + (flags,),
        (block, block, jax.ShapeDtypeStruct((peers * cap, 2 * LANES), BF16), side, side),
        [pltpu.VMEM((2 * rows, peers * cap), BF16)],
        2,
        after,
        held=(0, 1, 2, 3),
        in_smem=(4,),
        left=range(5),
    )


def inner_flow(first, last, data, place, lines, flags, peers, cap):
    rows, cols = first.shape[0], lines[0].shape[1]
    line = floats(4 * WIDE, cols)

    def body(*refs):
        inner_kernel(peers, cap, *refs)

    return staged(
        body,
        "inner_flow",
        (first, last, data, place) + tuple(lines) + (flags,),
        (floats(rows, cols), line, line),
        [pltpu.VMEM((rows * (cols // LANES - 2), peers * cap), BF16)],
        2,
        held=range(6),
        in_smem=(6,),
        left=range(3),
    )


def derive_kernel(take, outs, give):
    initial_ref, transmit_ref, share_ref, *edge_refs = outs
    rows, cols = initial_ref.shape
    flags = take(3)
    head = take(0)[...]
    share = take(2)[...].astype(F32)
    initial_ref[...] = head * share
    share_ref[...] = share
    transmit_ref[...] = take(1)[...] * (1.0 + 0.5 * jnp.tanh(head))
    for at, x in enumerate((initial_ref, transmit_ref, share_ref)):
        sent = sides_of(x[:, :LANES], x[:, cols - LANES :], flags[4])
        sent = sent + ordered(flags[5], x[:WIDE, :], x[rows - WIDE :, :])
        for ref, y in zip(edge_refs, sent):
            ref[at * WIDE : (at + 1) * WIDE, :] = y


def derive(head, trans_coef, land, flags):
    rows, cols = head.shape
    tile, side, line = floats(rows, cols), floats(3 * WIDE, rows), floats(3 * WIDE, cols)
    return staged(
        derive_kernel,
        "derive_tile",
        (head, trans_coef, land, flags),
        (tile, tile, tile, side, side, line, line),
        [],
        2,
        in_smem=(3,),
        left=range(7),
    )


def partners(axis):
    count = lax.axis_size(axis)
    return [(i, i ^ 1) for i in range(count)], [(i, (i + (1 if i % 2 else -1)) % count) for i in range(count)]


def swap(sides, axis):
    return tuple(lax.ppermute(x, axis, pairs) for x, pairs in zip(sides, partners(axis)))


def with_corners(lines, got):
    rows = got[0].shape[1]
    even = lax.axis_index("row") % 2 == 0
    ends = [(x[:, :LANES], x[:, rows - LANES :]) for x in got]
    to_first = [jnp.where(even, bottom, top) for top, bottom in ends]
    to_second = [jnp.where(even, top, bottom) for top, bottom in ends]
    return jnp.concatenate([lines[0], *to_first], axis=1), jnp.concatenate([lines[1], *to_second], axis=1)


def relax_kernel(take, outs, give, flow_ref, initial_ref, trans_ref, share_ref, next_ref, *weight_refs):
    (out_ref,) = outs
    rows, cols = out_ref.shape
    count = cols // LANES
    top, height = PAD, rows + 2 * EDGE
    one, flags = take(0)[0], take(1)
    ok_above, ok_below, ok_left, ok_right = [flags[i] for i in range(4)]
    from_right, from_left = ordered(flags[4], take(7)[...], take(6)[...])
    from_below, from_above = ordered(flags[5], take(9)[...], take(8)[...])
    fields = (flow_ref, initial_ref, trans_ref, share_ref)
    lane = iota((LANES, LANES), 1)

    def beside(left, right):
        many = len(fields) * WIDE
        fill = jnp.zeros((LANES - 2 * many, LANES), F32)
        block = jnp.transpose(jnp.concatenate([left, right, fill], axis=0))
        out = []
        for at in range(len(fields)):
            on_left = pltpu.roll(block, (LANES - WIDE - at * WIDE) % LANES, 1) * ok_left
            on_right = pltpu.roll(block, (-many - at * WIDE) % LANES, 1) * ok_right
            out.append(jnp.where(lane < WIDE, on_right, jnp.where(lane >= LANES - WIDE, on_left, 0.0)))
        return out

    first_row, last_row = top + EDGE, top + EDGE + rows
    for first in range(0, rows, LANES):
        blocks = beside(from_left[:, first : first + LANES], from_right[:, first : first + LANES])
        for ref, block in zip(fields, blocks):
            ref[count, first_row + first : first_row + first + LANES, :] = block
    corners = []
    for line in (from_above, from_below):
        on_right, on_left = ordered(flags[4], line[:, cols + LANES :], line[:, cols : cols + LANES])
        corners.append(beside(on_left, on_right))
    above, below = corners
    empty = jnp.zeros((PAD + EDGE, LANES), F32)
    for at, ref in enumerate(fields):
        part = slice(at * WIDE, (at + 1) * WIDE)
        for b in range(count + 1):
            ref[b, :first_row, :] = empty
            ref[b, last_row:, :] = empty
        before, after = slice(first_row - WIDE, first_row), slice(last_row, last_row + WIDE)
        ref[count, before, :] = above[at][LANES - WIDE :, :] * ok_above
        ref[count, after, :] = below[at][:WIDE, :] * ok_below
        for b in range(count):
            ref[b, before, :] = from_above[part, b * LANES : (b + 1) * LANES] * ok_above
            ref[b, after, :] = from_below[part, b * LANES : (b + 1) * LANES] * ok_below
    for b in range(count + 1):
        next_ref[b, :first_row, :] = empty
        next_ref[b, last_row:, :] = empty
    for ref, tile in ((flow_ref, take(5)), (trans_ref, take(2)), (share_ref, take(3)), (initial_ref, take(4))):
        for b in range(count):
            ref[b, first_row:last_row, :] = tile[:, b * LANES : (b + 1) * LANES].astype(F32)

    edge = iota((height, LANES), 1)

    def around(ref):
        mid = [ref[b, top : top + height, :] for b in range(count + 1)]
        later = [pltpu.roll(x, 1, 1) for x in mid]
        sooner = [pltpu.roll(x, LANES - 1, 1) for x in mid]
        for b in range(count + 1):
            yield (
                mid[b],
                ref[b, pl.ds(top - one, height), :],
                ref[b, pl.ds(top + one, height), :],
                jnp.where(edge == 0, later[b - 1], later[b]),
                jnp.where(edge == LANES - 1, sooner[(b + 1) % (count + 1)], sooner[b]),
            )

    up_ref, down_ref, left_ref, right_ref = weight_refs
    line = slice(top, top + height)
    for b, (mid, *others) in enumerate(around(trans_ref)):
        sums = [mid + x for x in others]
        total = 0.5 * (sums[0] + sums[1] + sums[2] + sums[3])
        scale = share_ref[b, line, :] / (store_rate + total)
        half = 0.5 * scale
        for ref, x in zip(weight_refs, sums):
            ref[b] = half * x
        flow_ref[b, line, :] = scale * (store_rate * initial_ref[b, line, :] + flow_ref[b, line, :])
    now, later_ref = initial_ref, next_ref
    for sweep in range(SWEEPS):
        for b, (_, above, below, on_left, on_right) in enumerate(around(now)):
            if sweep == SWEEPS - 1 and b == count:
                continue
            inflow = up_ref[b] * above + down_ref[b] * below
            inflow = inflow + left_ref[b] * on_left + right_ref[b] * on_right
            surface = flow_ref[b, line, :] + inflow
            if sweep == SWEEPS - 1:
                out_ref[:, b * LANES : (b + 1) * LANES] = surface[EDGE : EDGE + rows, :]
                give(0, b)
            else:
                later_ref[b, line, :] = surface
        now, later_ref = later_ref, now


def relax(flags, transmit, land_share, initial, flow, sides):
    rows, cols = flow.shape
    many = cols // LANES + 1
    field = pltpu.VMEM((many, rows + 2 * (EDGE + PAD), LANES), F32)
    weight = pltpu.VMEM((many, rows + 2 * EDGE, LANES), F32)
    one = jnp.where(flags[:1] < 2.0, 1, 0).astype(jnp.int32)
    return staged(
        relax_kernel,
        "lateral_relax",
        (one, flags, transmit, land_share, initial, flow) + tuple(sides),
        (floats(rows, cols),),
        [field] * 5 + [weight] * 4,
        6,
        held=range(2, 10),
        in_smem=(0, 1),
        pieces=(cols // LANES,),
        by_lanes=True,
    )[0]


def on_device(precip, head, trans_coef, land, dest, moisture, ksat):
    rows, cols = precip.shape
    row_count = lax.axis_size("row")
    col_count = lax.axis_size("col")
    peers = row_count * col_count
    owned, layers, _ = moisture.shape
    cap = 2 * (rows * cols // LANES) // peers
    axes = ("row", "col")
    moist2 = moisture.reshape(owned * layers, LANES)

    sent, place = pack(dest, precip, head, land, peers, cap, owned)
    wide = (2 * cap + 1) * LANES
    got = lax.all_to_all(sent.reshape(peers, 1, wide), axes, split_axis=0, concat_axis=0, tiled=True)
    got = got.reshape(peers * (2 * cap + 1), LANES)

    row_at, col_at = lax.axis_index("row"), lax.axis_index("col")
    flags = [row_at > 0, row_at < row_count - 1, col_at > 0, col_at < col_count - 1, col_at % 2 == 0, row_at % 2 == 0]
    flags = jnp.stack(flags).astype(F32)
    initial, transmit, land_share, *edges = derive(head, trans_coef, land, flags)
    responses = response(moist2, ksat, layers)

    infil, share, answer = owner_side(got, responses, peers, cap, (edges[0],))
    back = lax.all_to_all(answer.reshape(peers, cap, LANES), axes, split_axis=0, concat_axis=0, tiled=True)
    back = back.reshape(peers * cap, LANES)
    saturation = saturate(moist2, ksat, infil, share, layers)

    first, last, data, *sides = outer_flow(back, place, edges[:2], flags, cols, peers, cap, (saturation,))
    got_sides = swap(sides, "col")
    flow, *lines = inner_flow(first, last, data, place, edges[2:], flags, peers, cap)
    got_lines = swap(with_corners(lines, got_sides), "row")
    surface = relax(flags, transmit, land_share, initial, flow, got_sides + got_lines)
    return (saturation.reshape(owned, layers, LANES), surface)


def solution(mesh):
    tile = P("row", "col")
    return jax.shard_map(
        on_device,
        mesh=mesh,
        in_specs=(tile,) * 5 + (P(("row", "col"), None, None), P(("row", "col"), None)),
        out_specs=(P(("row", "col"), None, None), tile),
        check_vma=False,
    )
```

```python
import math

import jax
import jax.numpy as jnp
from jax import lax
from jax.experimental import pallas as pl
from jax.experimental.pallas import tpu as pltpu
from jax.sharding import PartitionSpec as P

SWEEPS = 4
LANES = 128
EDGE = 8
WIDE = 4
PAD = 8
GROUPS = 8

layer_depth = 0.1
step_ratio = 0.1
residual_water = 0.05
pore_range = 0.4
couple_rate = 0.05
recharge_gain = 20.0
store_rate = 0.2

F32 = jnp.float32
BF16 = jnp.bfloat16
MIB = 1 << 20


def iota(shape, dim):
    return lax.broadcasted_iota(jnp.int32, shape, dim)


def params():
    return pltpu.CompilerParams(vmem_limit_bytes=24 * MIB)


def cost(us):
    return pl.CostEstimate(flops=0, bytes_accessed=int(us * 3.0e6), transcendentals=0)


def halves(x):
    high = x.astype(BF16)
    low = (x - high.astype(F32)).astype(BF16)
    return high, low


def hbm(x):
    return pltpu.with_memory_space_constraint(x, pltpu.HBM)


def vmem(x):
    return pltpu.with_memory_space_constraint(x, pltpu.VMEM)


def staged(body, name, ins, outs, scratch, us, after=(), held=(), left=(), pieces=None, by_lanes=False, in_smem=(), small=False):
    n, m, k = len(ins), len(outs), len(after)
    pieces = pieces or (1,) * m
    moved = [i for i in range(n) if i not in held and i not in in_smem]
    sent = [i for i in range(m) if i not in left]

    def kernel(*refs):
        in_at, out_at = refs[:n], refs[n + k : n + k + m]
        rest = refs[n + k + m :]
        in_ref = dict(zip(moved, rest))
        rest = rest[len(moved) :]
        out_ref = dict(enumerate(out_at)) | dict(zip(sent, rest))
        rest = rest[len(sent) :]
        in_sem, out_sem = rest[:2]
        reads = {i: pltpu.make_async_copy(in_at[i], in_ref[i], in_sem.at[i]) for i in moved}
        writes = {}
        for i in sent:
            size = outs[i].shape[by_lanes] // pieces[i]
            for p in range(pieces[i]):
                part = pl.ds(p * size, size)
                part = (slice(None), part) if by_lanes else part
                sem = out_sem.at[sum(pieces[:i]) + p]
                writes[i, p] = pltpu.make_async_copy(out_ref[i].at[part], out_at[i].at[part], sem)
        for read in reads.values():
            read.start()

        def take(i):
            if i not in moved:
                return in_at[i]
            reads[i].wait()
            return in_ref[i]

        body(take, [out_ref[i] for i in range(m)], lambda i, p=0: writes[i, p].start(), *rest[2:])
        for write in writes.values():
            write.wait()

    spaces = {**{i: pltpu.VMEM for i in held}, **{i: pltpu.SMEM for i in in_smem}}
    in_specs = [pl.BlockSpec(memory_space=spaces.get(i, pltpu.HBM)) for i in range(n)]
    placed = [x if i in in_smem else vmem(x) if i in held else hbm(x) for i, x in enumerate(ins)]
    return pl.pallas_call(
        kernel,
        out_shape=tuple(
            pltpu.VMEM(x.shape, x.dtype) if i in left else pltpu.HBM(x.shape, x.dtype) for i, x in enumerate(outs)
        ),
        in_specs=in_specs + [pl.BlockSpec(memory_space=pltpu.VMEM if small else pltpu.HBM)] * k,
        out_specs=tuple(pl.BlockSpec(memory_space=pltpu.VMEM if i in left else pltpu.HBM) for i in range(m)),
        scratch_shapes=[pltpu.VMEM(ins[i].shape, ins[i].dtype) for i in moved]
        + [pltpu.VMEM(outs[i].shape, outs[i].dtype) for i in sent]
        + [pltpu.SemaphoreType.DMA((n,)), pltpu.SemaphoreType.DMA((sum(pieces),))]
        + list(scratch),
        compiler_params=pltpu.CompilerParams(vmem_limit_bytes=40 * MIB),
        cost_estimate=cost(us),
        name=name,
    )(*placed, *[vmem(x) if small else hbm(x) for x in after])


def floats(*shape):
    return jax.ShapeDtypeStruct(shape, F32)


def pack_kernel(peers, cap, owned, rows, cols, take, outs, give, hot_ref, data_ref):
    out_ref, place_ref = outs
    parts = cols // LANES
    blocks = rows * parts
    stride = 2 * cap + 1
    dest_ref = take(0)
    dest = jnp.concatenate([dest_ref[k : k + 1, :] for k in range(parts)], axis=1)
    shift = owned.bit_length() - 1
    owner = dest >> shift
    label = (dest & (owned - 1)) + 1
    owner_hot = owner == iota((peers, blocks), 0)
    before = (iota((LANES, LANES), 0) < iota((LANES, LANES), 1)).astype(F32).astype(BF16)
    carry = jnp.zeros((peers, 1), F32)
    ranks = []
    for chunk in range(blocks // LANES):
        hot = owner_hot[:, chunk * LANES : (chunk + 1) * LANES]
        hot_f = hot.astype(F32)
        count = jnp.dot(hot_f.astype(BF16), before, preferred_element_type=F32) + carry
        ranks.append(jnp.sum(count * hot_f, axis=0, keepdims=True))
        carry = carry + jnp.sum(hot_f, axis=1, keepdims=True)
    rank = jnp.concatenate(ranks, axis=1).astype(jnp.int32)
    place = owner + peers * rank
    place_ref[...] = place
    owner_f = owner_hot.astype(F32)
    rank_hot = (rank == iota((LANES, blocks), 0)).astype(F32).astype(BF16)
    contract = (((1,), (1,)), ((), ()))
    tops = (owner_f * (label >> 5).astype(F32)).astype(BF16)
    lows = (owner_f * (label & 31).astype(F32)).astype(BF16)
    labels = 32.0 * lax.dot_general(tops, rank_hot, contract, preferred_element_type=F32)
    labels = labels + lax.dot_general(lows, rank_hot, contract, preferred_element_type=F32)
    out_ref[pl.ds(2 * cap, peers, stride=stride), :] = labels
    size = peers // GROUPS

    def mark(group):
        for k in range(cap):
            at = (group * cap + k) * size
            hot_ref[at : at + size, :] = (
                (place == iota((size, blocks), 0) + (k * peers + group * size)).astype(F32).astype(BF16)
            )

    mark(0)
    precip_ref, head_ref, land_ref = take(1), take(2), take(3)
    for part in range(parts):
        lane = slice(part * LANES, (part + 1) * LANES)
        line = slice(part * rows, (part + 1) * rows)
        infil = precip_ref[:, lane] * land_ref[:, lane].astype(F32)
        for at, piece in enumerate(halves(infil) + halves(head_ref[:, lane])):
            data_ref[line, at * LANES : (at + 1) * LANES] = piece
    for group in range(GROUPS):
        if group + 1 < GROUPS:
            mark(group + 1)
        line = slice(group * cap * size, (group + 1) * cap * size)
        moved = jnp.dot(hot_ref[line, :], data_ref[...], preferred_element_type=F32)
        for k in range(cap):
            part = moved[k * size : (k + 1) * size]
            row = group * size * stride + k
            out_ref[pl.ds(row, size, stride=stride), :] = part[:, :LANES] + part[:, LANES : 2 * LANES]
            out_ref[pl.ds(row + cap, size, stride=stride), :] = part[:, 2 * LANES : 3 * LANES] + part[:, 3 * LANES :]
        give(0, group)


def pack(dest, precip, head, land, peers, cap, owned):
    rows, cols = precip.shape
    blocks = rows * cols // LANES

    def body(*refs):
        pack_kernel(peers, cap, owned, rows, cols, *refs)

    return staged(
        body,
        "pack_forcing",
        (jnp.transpose(dest), precip, head, land),
        (floats(peers * (2 * cap + 1), LANES), jax.ShapeDtypeStruct((1, blocks), jnp.int32)),
        [pltpu.VMEM((peers * cap, blocks), BF16), pltpu.VMEM((blocks, 4 * LANES), BF16)],
        5,
        pieces=(GROUPS, 1),
        left=(1,),
    )


def layer_terms(moist, half_k, depth_factor):
    wet = moist * (1.0 / pore_range) - residual_water / pore_range
    wet2 = wet * wet
    a = half_k * depth_factor
    t = a * wet2
    return wet, 7.5 * t, t * wet, a + 5.0 * t


def inverse(x):
    return 1.0 / x


def eliminate(layers, load, ksat, infil, response, keep):
    half_k = 0.5 * ksat
    moist = load(0)
    wet, hs, hc, d5 = layer_terms(moist, half_k, math.exp(-0.5 * layer_depth))
    flux_above = infil
    ratio = reduced = resp = hs_prev = g_prev = None
    for k in range(layers):
        last = k == layers - 1
        if not last:
            moist_n = load(k + 1)
            wet_n, hs_n, hc_n, d5_n = layer_terms(
                moist_n, half_k, math.exp(-(k + 1.5) * layer_depth)
            )
            g = d5 + d5_n
            flux = (hc + hc_n) - g * (moist_n - moist)
        if k == 0:
            diagonal = (g + step_ratio) + hs
        elif last:
            diagonal = (g_prev + (step_ratio + couple_rate)) + hs
        else:
            diagonal = (g_prev + step_ratio) + g
        if last:
            bottom = 2.0 * hc + couple_rate * (moist - residual_water)
            right = flux_above - bottom
        else:
            right = (0.0 - flux) if flux_above is None else (flux_above - flux)
        if k == 0:
            inv = inverse(diagonal)
            reduced = right * inv
            resp = inv
        else:
            neg_sub = hs_prev + g_prev
            inv = inverse(diagonal + neg_sub * ratio)
            reduced = (right + neg_sub * reduced) * inv
            if response:
                resp = neg_sub * resp * inv
        if last:
            return bottom, 2.0 * hs + couple_rate, reduced, resp, inv, wet
        ratio = (hs_n - g) * inv
        if keep is not None:
            keep(k, wet, ratio, reduced)
        hs_prev, g_prev = hs, g
        flux_above = flux
        moist, wet, hs, hc, d5 = moist_n, wet_n, hs_n, hc_n, d5_n


def response_kernel(layers, chunk, moist_ref, ksat_ref, alpha_ref, beta_ref, gamma_ref):
    def step(j, carry):
        base = j * (chunk * layers)
        line = pl.ds(j * chunk, chunk)
        load = lambda k: moist_ref[pl.ds(base + k, chunk, stride=layers), :]
        bottom, gain, reduced, resp, inv, _ = eliminate(layers, load, ksat_ref[line, :], None, True, None)
        alpha_ref[line, :] = bottom + gain * reduced
        beta_ref[line, :] = gain * resp
        gamma_ref[line, :] = (couple_rate * pore_range) * (gain * inv - 1.0)
        return carry

    lax.fori_loop(0, ksat_ref.shape[0] // chunk, step, 0)


def response(moist2, ksat, layers):
    owned = ksat.shape[0]
    size = 128

    def kernel(*refs):
        response_kernel(layers, 128, *refs)

    small = pl.BlockSpec((size, LANES), lambda i: (i, 0))
    return pl.pallas_call(
        kernel,
        grid=(owned // size,),
        out_shape=(pltpu.HBM((owned, LANES), F32),) * 3,
        in_specs=[pl.BlockSpec((size * layers, LANES), lambda i: (i, 0)), small],
        out_specs=(small,) * 3,
        compiler_params=params(),
        cost_estimate=cost(13),
        name="column_response",
    )(hbm(moist2), hbm(ksat))


def saturation_kernel(layers, chunk, moist_ref, ksat_ref, infil_ref, share_ref, out_ref, wet_s, ratio_s, reduced_s):
    def step(j, carry):
        base = j * (chunk * layers)
        line = pl.ds(j * chunk, chunk)
        load = lambda k: moist_ref[pl.ds(base + k, chunk, stride=layers), :]

        def keep(k, wet, ratio, reduced):
            wet_s[k] = wet
            ratio_s[k] = ratio
            reduced_s[k] = reduced

        _, _, reduced, _, inv, wet = eliminate(layers, load, ksat_ref[line, :], infil_ref[line, :], False, keep)
        change = reduced + (couple_rate * pore_range) * share_ref[line, :] * inv
        out_ref[pl.ds(base + layers - 1, chunk, stride=layers), :] = wet + (1.0 / pore_range) * change
        for k in range(layers - 2, -1, -1):
            change = reduced_s[k] - ratio_s[k] * change
            out_ref[pl.ds(base + k, chunk, stride=layers), :] = wet_s[k] + (1.0 / pore_range) * change
        return carry

    lax.fori_loop(0, ksat_ref.shape[0] // chunk, step, 0)


def saturate(moist2, ksat, infil, share, layers):
    owned = ksat.shape[0]
    size, chunk = 128, 32

    def kernel(*refs):
        saturation_kernel(layers, chunk, *refs)

    small = pl.BlockSpec((size, LANES), lambda i: (i, 0))
    large = pl.BlockSpec((size * layers, LANES), lambda i: (i, 0))
    return pl.pallas_call(
        kernel,
        grid=(owned // size,),
        out_shape=pltpu.HBM((owned * layers, LANES), F32),
        in_specs=[large, small, small, small],
        out_specs=large,
        scratch_shapes=[pltpu.VMEM((layers - 1, chunk, LANES), F32)] * 3,
        compiler_params=params(),
        cost_estimate=cost(14),
        name="column_saturation",
    )(*[hbm(x) for x in (moist2, ksat, infil, share)])


def owner_kernel(peers, cap, owned, take, outs, give, data_ref, hot_ref, back_ref, rech_ref):
    infil_ref, share_ref, ans_ref = outs
    got_ref = take(0)
    stride = 2 * cap + 1
    labels = got_ref[pl.ds(2 * cap, peers, stride=stride), :]
    turned = jnp.transpose(labels).astype(jnp.int32) - 1
    labels = labels.astype(jnp.int32) - 1
    group = owned // 2

    def mark(first):
        for k in range(cap):
            hot_ref[first : first + group, k * peers : (k + 1) * peers] = (
                (turned[k : k + 1, :] == iota((group, peers), 0) + first).astype(F32).astype(BF16)
            )

    for k in range(cap):
        line = slice(k * peers, (k + 1) * peers)
        pieces = halves(got_ref[pl.ds(k, peers, stride=stride), :])
        pieces = pieces + halves(got_ref[pl.ds(cap + k, peers, stride=stride), :])
        for at, piece in enumerate(pieces):
            data_ref[line, at * LANES : (at + 1) * LANES] = piece
    size = peers // GROUPS

    def mark_back(first):
        for k in range(cap):
            at = first * cap + k * size
            back_ref[at : at + size, :] = (
                (labels[first : first + size, k : k + 1] == iota((size, owned), 1)).astype(F32).astype(BF16)
            )

    mark(0)
    for first in range(0, owned, group):
        line = slice(first, first + group)
        if first + group < owned:
            mark(first + group)
        moved = jnp.dot(hot_ref[line, :], data_ref[...], preferred_element_type=F32)
        infil_ref[line, :] = moved[:, :LANES] + moved[:, LANES : 2 * LANES]
        share_ref[line, :] = jax.nn.sigmoid(moved[:, 2 * LANES : 3 * LANES] + moved[:, 3 * LANES :])
    alpha_ref, beta_ref, gamma_ref = [take(1 + k) for k in range(3)]
    rech = alpha_ref[...] + beta_ref[...] * infil_ref[...] + gamma_ref[...] * share_ref[...]
    high, low = halves(rech)
    rech_ref[:, :LANES] = high
    rech_ref[:, LANES:] = low
    mark_back(0)
    for turn in range(GROUPS):
        first = turn * size
        if turn + 1 < GROUPS:
            mark_back(first + size)
        line = slice(first * cap, (first + size) * cap)
        moved = jnp.dot(back_ref[line, :], rech_ref[...], preferred_element_type=F32)
        for k in range(cap):
            part = moved[k * size : (k + 1) * size]
            ans_ref[pl.ds(first * cap + k, size, stride=cap), :] = part[:, :LANES] + part[:, LANES:]
        if turn == 1:
            give(2, 0)
            give(2, 1)
            give(0)
            give(1)
        if turn > 1:
            give(2, turn)


def owner_side(got, responses, peers, cap, after):
    owned = responses[0].shape[0]

    def body(*refs):
        owner_kernel(peers, cap, owned, *refs)

    return staged(
        body,
        "owner_side",
        (got,) + tuple(responses),
        (floats(owned, LANES), floats(owned, LANES), floats(peers * cap, LANES)),
        [
            pltpu.VMEM((peers * cap, 4 * LANES), BF16),
            pltpu.VMEM((owned, peers * cap), BF16),
            pltpu.VMEM((peers * cap, owned), BF16),
            pltpu.VMEM((owned, 2 * LANES), BF16),
        ],
        8,
        after,
        held=(0,),
        pieces=(1, 1, GROUPS),
        small=True,
    )


def ordered(even, low, high):
    odd = 1.0 - even
    return even * high + odd * low, even * low + odd * high


def sides_of(first, last, even):
    return ordered(even, jnp.transpose(first)[:WIDE, :], jnp.transpose(last)[LANES - WIDE :, :])


def unpack(place_f, data_ref, hot_ref, blocks, peers, cap):
    eye = iota((LANES, LANES), 0) == iota((LANES, LANES), 1)
    for first in range(0, blocks, LANES):
        column = jnp.sum(jnp.where(eye, place_f[:, first : first + LANES], 0.0), axis=1, keepdims=True)
        column = column.astype(jnp.int32)
        for k in range(cap):
            hot_ref[first : first + LANES, k * peers : (k + 1) * peers] = (
                (column == iota((LANES, peers), 1) + k * peers).astype(F32).astype(BF16)
            )
    moved = jnp.dot(hot_ref[:blocks, :], data_ref[...], preferred_element_type=F32)
    return recharge_gain * (moved[:, :LANES] + moved[:, LANES:])


def outer_kernel(peers, cap, rows, cols, take, outs, give, hot_ref):
    first_ref, last_ref, data_ref, *edge_refs = outs
    back_ref = take(0)
    for k in range(cap):
        line = slice(k * peers, (k + 1) * peers)
        high, low = halves(back_ref[pl.ds(k, peers, stride=cap), :])
        data_ref[line, :LANES] = high
        data_ref[line, LANES:] = low
    place_f = take(1)[...].astype(F32)
    flags = take(4)
    last_at = rows * (cols // LANES - 1)
    first = unpack(place_f[:, :rows], data_ref, hot_ref.at[:rows], rows, peers, cap)
    last = unpack(place_f[:, last_at:], data_ref, hot_ref.at[rows:], rows, peers, cap)
    first_ref[...] = first
    last_ref[...] = last
    for ref, raw, x in zip(edge_refs, (take(2), take(3)), sides_of(first, last, flags[4])):
        ref[...] = jnp.concatenate([x, raw[...]], axis=0)


def inner_kernel(peers, cap, take, outs, give, hot_ref):
    flow_ref, *edge_refs = outs
    rows, cols = flow_ref.shape
    first_ref, last_ref, data_ref = take(0), take(1), take(2)
    flags = take(6)
    flow_ref[:, :LANES] = first_ref[...]
    flow_ref[:, cols - LANES :] = last_ref[...]
    place_f = take(3)[...].astype(F32)
    for part in range(1, cols // LANES - 1):
        at = (part - 1) * rows
        flow_ref[:, part * LANES : (part + 1) * LANES] = unpack(
            place_f[:, part * rows : (part + 1) * rows], data_ref, hot_ref.at[at : at + rows], rows, peers, cap
        )
    lines = ordered(flags[5], flow_ref[:WIDE, :], flow_ref[rows - WIDE :, :])
    for ref, raw, x in zip(edge_refs, (take(4), take(5)), lines):
        ref[...] = jnp.concatenate([x, raw[...]], axis=0)


def outer_flow(back, place, sides, flags, cols, peers, cap, after):
    rows = sides[0].shape[1]
    block, side = floats(rows, LANES), floats(4 * WIDE, rows)

    def body(*refs):
        outer_kernel(peers, cap, rows, cols, *refs)

    return staged(
        body,
        "outer_flow",
        (back, place) + tuple(sides) + (flags,),
        (block, block, jax.ShapeDtypeStruct((peers * cap, 2 * LANES), BF16), side, side),
        [pltpu.VMEM((2 * rows, peers * cap), BF16)],
        2,
        after,
        held=(0, 1, 2, 3),
        in_smem=(4,),
        left=range(5),
    )


def inner_flow(first, last, data, place, lines, flags, peers, cap):
    rows, cols = first.shape[0], lines[0].shape[1]
    line = floats(4 * WIDE, cols)

    def body(*refs):
        inner_kernel(peers, cap, *refs)

    return staged(
        body,
        "inner_flow",
        (first, last, data, place) + tuple(lines) + (flags,),
        (floats(rows, cols), line, line),
        [pltpu.VMEM((rows * (cols // LANES - 2), peers * cap), BF16)],
        2,
        held=range(6),
        in_smem=(6,),
        left=range(3),
    )


def derive_kernel(take, outs, give):
    initial_ref, transmit_ref, share_ref, *edge_refs = outs
    rows, cols = initial_ref.shape
    flags = take(3)
    head = take(0)[...]
    share = take(2)[...].astype(F32)
    initial_ref[...] = head * share
    share_ref[...] = share
    transmit_ref[...] = take(1)[...] * (1.0 + 0.5 * jnp.tanh(head))
    for at, x in enumerate((initial_ref, transmit_ref, share_ref)):
        sent = sides_of(x[:, :LANES], x[:, cols - LANES :], flags[4])
        sent = sent + ordered(flags[5], x[:WIDE, :], x[rows - WIDE :, :])
        for ref, y in zip(edge_refs, sent):
            ref[at * WIDE : (at + 1) * WIDE, :] = y


def derive(head, trans_coef, land, flags):
    rows, cols = head.shape
    tile, side, line = floats(rows, cols), floats(3 * WIDE, rows), floats(3 * WIDE, cols)
    return staged(
        derive_kernel,
        "derive_tile",
        (head, trans_coef, land, flags),
        (tile, tile, tile, side, side, line, line),
        [],
        2,
        in_smem=(3,),
        left=range(7),
    )


def partners(axis):
    count = lax.axis_size(axis)
    return [(i, i ^ 1) for i in range(count)], [(i, (i + (1 if i % 2 else -1)) % count) for i in range(count)]


def swap(sides, axis):
    return tuple(lax.ppermute(x, axis, pairs) for x, pairs in zip(sides, partners(axis)))


def with_corners(lines, got):
    rows = got[0].shape[1]
    even = lax.axis_index("row") % 2 == 0
    ends = [(x[:, :LANES], x[:, rows - LANES :]) for x in got]
    to_first = [jnp.where(even, bottom, top) for top, bottom in ends]
    to_second = [jnp.where(even, top, bottom) for top, bottom in ends]
    return jnp.concatenate([lines[0], *to_first], axis=1), jnp.concatenate([lines[1], *to_second], axis=1)


def relax_kernel(take, outs, give, flow_ref, initial_ref, trans_ref, share_ref, next_ref, *weight_refs):
    (out_ref,) = outs
    rows, cols = out_ref.shape
    count = cols // LANES
    top, height = PAD, rows + 2 * EDGE
    one, flags = take(0)[0], take(1)
    ok_above, ok_below, ok_left, ok_right = [flags[i] for i in range(4)]
    from_right, from_left = ordered(flags[4], take(7)[...], take(6)[...])
    from_below, from_above = ordered(flags[5], take(9)[...], take(8)[...])
    fields = (flow_ref, initial_ref, trans_ref, share_ref)
    lane = iota((LANES, LANES), 1)

    def beside(left, right):
        many = len(fields) * WIDE
        fill = jnp.zeros((LANES - 2 * many, LANES), F32)
        block = jnp.transpose(jnp.concatenate([left, right, fill], axis=0))
        out = []
        for at in range(len(fields)):
            on_left = pltpu.roll(block, (LANES - WIDE - at * WIDE) % LANES, 1) * ok_left
            on_right = pltpu.roll(block, (-many - at * WIDE) % LANES, 1) * ok_right
            out.append(jnp.where(lane < WIDE, on_right, jnp.where(lane >= LANES - WIDE, on_left, 0.0)))
        return out

    first_row, last_row = top + EDGE, top + EDGE + rows
    for first in range(0, rows, LANES):
        blocks = beside(from_left[:, first : first + LANES], from_right[:, first : first + LANES])
        for ref, block in zip(fields, blocks):
            ref[count, first_row + first : first_row + first + LANES, :] = block
    corners = []
    for line in (from_above, from_below):
        on_right, on_left = ordered(flags[4], line[:, cols + LANES :], line[:, cols : cols + LANES])
        corners.append(beside(on_left, on_right))
    above, below = corners
    empty = jnp.zeros((PAD + EDGE, LANES), F32)
    for at, ref in enumerate(fields):
        part = slice(at * WIDE, (at + 1) * WIDE)
        for b in range(count + 1):
            ref[b, :first_row, :] = empty
            ref[b, last_row:, :] = empty
        before, after = slice(first_row - WIDE, first_row), slice(last_row, last_row + WIDE)
        ref[count, before, :] = above[at][LANES - WIDE :, :] * ok_above
        ref[count, after, :] = below[at][:WIDE, :] * ok_below
        for b in range(count):
            ref[b, before, :] = from_above[part, b * LANES : (b + 1) * LANES] * ok_above
            ref[b, after, :] = from_below[part, b * LANES : (b + 1) * LANES] * ok_below
    for b in range(count + 1):
        next_ref[b, :first_row, :] = empty
        next_ref[b, last_row:, :] = empty
    for ref, tile in ((flow_ref, take(5)), (trans_ref, take(2)), (share_ref, take(3)), (initial_ref, take(4))):
        for b in range(count):
            ref[b, first_row:last_row, :] = tile[:, b * LANES : (b + 1) * LANES].astype(F32)

    step = 16
    edge = iota((step, LANES), 1)

    def around(ref, row):
        mid = [ref[b, top + row : top + row + step, :] for b in range(count + 1)]
        later = [pltpu.roll(x, 1, 1) for x in mid]
        sooner = [pltpu.roll(x, LANES - 1, 1) for x in mid]
        for b in range(count + 1):
            yield (
                mid[b],
                ref[b, pl.ds(top + row - one, step), :],
                ref[b, pl.ds(top + row + one, step), :],
                jnp.where(edge == 0, later[b - 1], later[b]),
                jnp.where(edge == LANES - 1, sooner[(b + 1) % (count + 1)], sooner[b]),
            )

    for row in range(0, height, step):
        line = slice(top + row, top + row + step)
        for b, (mid, *others) in enumerate(around(trans_ref, row)):
            sums = [mid + x for x in others]
            total = 0.5 * (sums[0] + sums[1] + sums[2] + sums[3])
            scale = share_ref[b, line, :] / (store_rate + total)
            half = 0.5 * scale
            for ref, x in zip(weight_refs, sums):
                ref[b, row : row + step, :] = half * x
            flow_ref[b, line, :] = scale * (store_rate * initial_ref[b, line, :] + flow_ref[b, line, :])
    now, later_ref = initial_ref, next_ref
    piece = rows // 4
    for sweep in range(SWEEPS):
        final = sweep == SWEEPS - 1
        for row in range(EDGE, EDGE + rows, step) if final else range(0, height, step):
            part = slice(row, row + step)
            line = slice(top + row, top + row + step)
            for b, (_, *others) in enumerate(around(now, row)):
                if final and b == count:
                    continue
                up, down, left, right = [ref[b, part, :] * x for ref, x in zip(weight_refs, others)]
                surface = flow_ref[b, line, :] + ((up + down) + (left + right))
                if final:
                    out_ref[row - EDGE : row - EDGE + step, b * LANES : (b + 1) * LANES] = surface
                else:
                    later_ref[b, line, :] = surface
            if final and (row - EDGE + step) % piece == 0:
                give(0, (row - EDGE + step) // piece - 1)
        now, later_ref = later_ref, now


def relax(flags, transmit, land_share, initial, flow, sides):
    rows, cols = flow.shape
    many = cols // LANES + 1
    field = pltpu.VMEM((many, rows + 2 * (EDGE + PAD), LANES), F32)
    weight = pltpu.VMEM((many, rows + 2 * EDGE, LANES), F32)
    one = jnp.where(flags[:1] < 2.0, 1, 0).astype(jnp.int32)
    return staged(
        relax_kernel,
        "lateral_relax",
        (one, flags, transmit, land_share, initial, flow) + tuple(sides),
        (floats(rows, cols),),
        [field] * 5 + [weight] * 4,
        6,
        held=range(2, 10),
        in_smem=(0, 1),
        pieces=(4,),
    )[0]


def on_device(precip, head, trans_coef, land, dest, moisture, ksat):
    rows, cols = precip.shape
    row_count = lax.axis_size("row")
    col_count = lax.axis_size("col")
    peers = row_count * col_count
    owned, layers, _ = moisture.shape
    cap = 2 * (rows * cols // LANES) // peers
    axes = ("row", "col")
    moist2 = moisture.reshape(owned * layers, LANES)

    sent, place = pack(dest, precip, head, land, peers, cap, owned)
    wide = (2 * cap + 1) * LANES
    got = lax.all_to_all(sent.reshape(peers, 1, wide), axes, split_axis=0, concat_axis=0, tiled=True)
    got = got.reshape(peers * (2 * cap + 1), LANES)

    row_at, col_at = lax.axis_index("row"), lax.axis_index("col")
    flags = [row_at > 0, row_at < row_count - 1, col_at > 0, col_at < col_count - 1, col_at % 2 == 0, row_at % 2 == 0]
    flags = jnp.stack(flags).astype(F32)
    initial, transmit, land_share, *edges = derive(head, trans_coef, land, flags)
    responses = response(moist2, ksat, layers)

    infil, share, answer = owner_side(got, responses, peers, cap, (edges[0],))
    back = lax.all_to_all(answer.reshape(peers, cap, LANES), axes, split_axis=0, concat_axis=0, tiled=True)
    back = back.reshape(peers * cap, LANES)
    saturation = saturate(moist2, ksat, infil, share, layers)

    first, last, data, *sides = outer_flow(back, place, edges[:2], flags, cols, peers, cap, (saturation,))
    got_sides = swap(sides, "col")
    flow, *lines = inner_flow(first, last, data, place, edges[2:], flags, peers, cap)
    got_lines = swap(with_corners(lines, got_sides), "row")
    surface = relax(flags, transmit, land_share, initial, flow, got_sides + got_lines)
    return (saturation.reshape(owned, layers, LANES), surface)


def solution(mesh):
    tile = P("row", "col")
    return jax.shard_map(
        on_device,
        mesh=mesh,
        in_specs=(tile,) * 5 + (P(("row", "col"), None, None), P(("row", "col"), None)),
        out_specs=(P(("row", "col"), None, None), tile),
        check_vma=False,
    )
```
